32 devices in a mesh: grp: 2 (over x), dp: 2 (over core), tp: 8 (over z, y).
Axes of the slice: x: 2, y: 2, z: 4, core: 2. Of those that a mesh axis runs over, the one named last changes fastest.
Arguments:
- query_inputs: bfloat16 [4096, 8192], P(('grp', 'dp'), 'tp'), parts along dimension 0, may hold values from -250 to 250
- output_inputs: bfloat16 [4096, 8192], P(('grp', 'dp'), 'tp'), parts along dimension 0, may hold values from -250 to 250
- query_cotangent: bfloat16 [4096, 8192], P(('grp', 'dp'), 'tp'), parts along dimension 0, may hold values from -250 to 250
- output_cotangent: bfloat16 [4096, 8192], P(('grp', 'dp'), 'tp'), parts along dimension 0, may hold values from -250 to 250
- completion: int32 [4096], P(('grp', 'dp')), parts along dimension 0, may hold values from 0 to 15, never falling along the last dimension, each value on 1 to 256 neighbouring positions
- rewards: float32 [32], P('grp'), parts along dimension 0, may hold values from 0 to 1
- query_down: float32 [16384, 64], P(('grp', 'tp')), parts along dimension 0, may hold values from -0.0625 to 0.0625
- query_up: float32 [128, 8192], P('grp', 'tp'), parts along dimension 0, may hold values from -0.1875 to 0.1875
- output_down: float32 [16384, 64], P(('grp', 'tp')), parts along dimension 0, may hold values from -0.0625 to 0.0625
- output_up: float32 [128, 8192], P('grp', 'tp'), parts along dimension 0, may hold values from -0.1875 to 0.1875
- query_fixed_weight: bfloat16 [8192, 8192], P('dp', 'tp'), may hold values from -0.0625 to 0.0625
- output_fixed_weight: bfloat16 [8192, 8192], P('tp', 'dp'), may hold values from -0.09375 to 0.09375
- keyval_frozen: bfloat16 [8192, 2048], P('tp'), may hold values from -0.0625 to 0.0625
- decode_states: bfloat16 [4, 32, 8192], P(None, ('grp', 'dp'), 'tp'), parts along dimension 1, may hold values from -6 to 6
- key_cache: bfloat16 [32, 8, 64, 128], P(('grp', 'dp', 'tp')), parts along dimension 0, may hold values from -400 to 400
- value_cache: bfloat16 [32, 8, 64, 128], P(('grp', 'dp', 'tp')), parts along dimension 0, may hold values from -6 to 6
- cache_lengths: int32 [32], P(('grp', 'dp')), parts along dimension 0, may hold values from 2 to 64, as said below
Outputs:
- decoded: bfloat16 [4, 32, 8192], P(None, ('grp', 'dp'), 'tp'), parts along dimension 1
- new_query_down: float32 [16384, 64], P(('grp', 'tp')), parts along dimension 0
- new_query_up: float32 [128, 8192], P('grp', 'tp'), parts along dimension 0
- new_output_down: float32 [16384, 64], P(('grp', 'tp')), parts along dimension 0
- new_output_up: float32 [128, 8192], P('grp', 'tp'), parts along dimension 0
The draws below stay inside these ranges and needn't reach their ends.
There are 2 independent parts, one for each index of `grp`. The reference program is written for one: setup_inputs(seed, part) draws one part's arguments, and reference() takes and returns one part's arrays. A program takes and returns all parts, laid end to end along the dimension named above; an argument that names none is the same for every part. Nothing has to cross between parts.
Inputs may be any that keep to these rules, and one draw needn't show every extreme that they name: Tokens of one completion are contiguous and completion numbers never fall along the tokens; a completion has 1 to 256 tokens. Row r uses the cached positions below cache_lengths[r]; some row uses all 64.
All inputs are finite; a program needn't handle non-finite values.
Results may differ from the reference program's by a relative error of at most 0.028.
Values may be sent and summed in bfloat16 or wider, within the bound.
A program may use at most 192 MiB of HBM per device.

```python
import math
import jax
import jax.numpy as jnp
import numpy as np
from jax import lax

D = 8192
HEADS = 64
KVH = 8
HD = 128
RANK = 64
STEPS = 4
COMP = 16
CACHE = 64
DQ = 8192
TOKENS = 2048
ROWS = 16
MAXSEG = 256
N_TP = 8


def spread_field(values_base, key_rows, row_top):
    row_count, col_count = values_base.shape
    col_place = jnp.arange(col_count, dtype=jnp.float32) / col_count
    row_power = jax.random.uniform(key_rows, (row_count, 1), jnp.float32, 0.0, row_top)
    return 0.1 * values_base * jnp.power(10.0, row_power) * jnp.power(10.0, col_place)[None, :]


def draw_query_inputs(key, part):
    key = jax.random.fold_in(key, 3)
    key_base, key_rows = jax.random.split(key, 2)
    values_base = jnp.clip(jax.random.normal(key_base, (TOKENS, D), jnp.float32), -5.0, 5.0)
    return spread_field(values_base, key_rows, 1.0).astype(jnp.bfloat16)


def draw_output_inputs(key, part):
    key = jax.random.fold_in(key, 5)
    key_base, key_rows = jax.random.split(key, 2)
    values_base = jnp.clip(jax.random.normal(key_base, (TOKENS, DQ), jnp.float32), -5.0, 5.0)
    return spread_field(values_base, key_rows, 1.0).astype(jnp.bfloat16)


def draw_query_cotangent(key, part):
    key = jax.random.fold_in(key, 7)
    key_base, key_rows = jax.random.split(key, 2)
    values_base = jnp.clip(jax.random.normal(key_base, (TOKENS, DQ), jnp.float32), -5.0, 5.0)
    return spread_field(values_base, key_rows, 1.0).astype(jnp.bfloat16)


def draw_output_cotangent(key, part):
    key = jax.random.fold_in(key, 9)
    key_base, key_rows = jax.random.split(key, 2)
    values_base = jnp.clip(jax.random.normal(key_base, (TOKENS, D), jnp.float32), -5.0, 5.0)
    return spread_field(values_base, key_rows, 1.0).astype(jnp.bfloat16)


def draw_key_cache(key, part):
    key = jax.random.fold_in(key, 11)
    key_base = jax.random.fold_in(key, 0)
    cache_shape = (ROWS, KVH, CACHE, HD)
    drawn_keys = jnp.clip(jax.random.normal(key_base, cache_shape, jnp.float32), -6.0, 6.0)
    return drawn_keys.astype(jnp.bfloat16)


def draw_cache_lengths(key, part):
    key = jax.random.fold_in(key, 17)
    key_lengths, key_full = jax.random.split(key)
    drawn_lengths = jax.random.randint(key_lengths, (ROWS,), 2, CACHE + 1, dtype=jnp.int32)
    chosen = jax.random.randint(key_full, (), 0, ROWS, dtype=jnp.int32)
    return jnp.where(jnp.arange(ROWS, dtype=jnp.int32) == chosen, CACHE, drawn_lengths).astype(jnp.int32)


def spiked(values, rng, source, target, shards_of, factor):
    owner, partner = [(jnp.arange(values.shape[axis_at]) // (values.shape[axis_at] // shards_of)).reshape([-1 if axis == axis_at else 1 for axis in range(values.ndim)]) for axis_at in (source, target)]
    chosen = jax.random.permutation(rng, shards_of)[partner]
    strong = (owner == chosen) | (owner == (partner + shards_of // 2) % shards_of)
    return jnp.where(strong, factor * values, values)


def shard_levels(stream_key, extent, pieces, least, high):
    def one(axis_at, blocks):
        steps = jax.random.uniform(jax.random.fold_in(jax.random.fold_in(stream_key, 6), axis_at), (blocks,), jnp.float32, least / len(pieces), high / len(pieces))
        return jnp.repeat(jnp.exp(steps), extent[axis_at] // blocks).reshape((-1,) + (1,) * (len(extent) - axis_at - 1))

    gain = one(*pieces[0])
    for cut in pieces[1:]:
        gain = gain * one(*cut)
    return gain


def profile(number_of, total, most, lean):
    portions = [(1 << 20) // math.isqrt(rank ** lean) + 1 for rank in range(2, number_of + 1)]
    rest, holding = total - most - (number_of - 1), [1] * (number_of - 1)
    while rest > 0:
        candidates = [i for i in range(number_of - 1) if holding[i] < most]
        whole, left = sum([portions[i] for i in candidates]), rest
        for i in candidates:
            extra = min(most - holding[i], max(1, left * portions[i] // whole), rest)
            holding[i] = holding[i] + extra
            rest = rest - extra
    return np.array([most] + holding)


def ragged_sizes(rng, number_of, total, limit, skew):
    if number_of == 2:
        one = jax.random.randint(rng, (), max(1, total - limit), min(limit, total - 1) + 1)
        return jnp.stack([one, total - one])
    lengths = jnp.asarray(profile(number_of, total, limit, skew), jnp.int32)
    pairs = (number_of - 1) // 2
    giver, receiver = lengths[1:1 + 2 * pairs:2], lengths[2:2 + 2 * pairs:2]
    slack = jnp.minimum(giver - 1, limit - receiver)
    passed = jax.random.randint(jax.random.fold_in(rng, 1), (pairs,), 0, 1 << 20) % (slack + 1)
    lengths = lengths.at[1:1 + 2 * pairs:2].set(giver - passed).at[2:2 + 2 * pairs:2].set(receiver + passed)
    return lengths[jax.random.permutation(jax.random.fold_in(rng, 2), number_of)]


def scatter_about(own_key, dims, deviation, reach, cuts=(), held_as=jnp.bfloat16):
    factor_of = shard_levels(own_key, dims, cuts, -0.22, 0.18) if cuts else 1.0
    array = jax.random.normal(own_key, dims, jnp.float32) * deviation * factor_of
    return jnp.minimum(jnp.maximum(array, -reach), reach).astype(held_as)


def noise_with(rng, dims, spread, most, pieces, heavy, held_as=jnp.bfloat16):
    values = spread * jax.random.normal(rng, dims, jnp.float32)
    if pieces:
        values = values * shard_levels(rng, dims, pieces, -0.22, 0.18)
    return jnp.clip(spiked(values, jax.random.fold_in(rng, 3), *heavy), -most, most).astype(held_as)


def setup_inputs(seed: int = 0, part: int = 0) -> dict:
    splits = jax.random.split(jax.random.key(seed), 18)
    own_keys = jax.random.split(jax.random.fold_in(splits[17], part), 18)
    query_inputs = draw_query_inputs(jax.random.fold_in(jax.random.fold_in(splits[17], part), 71), part)
    output_inputs = draw_output_inputs(jax.random.fold_in(jax.random.fold_in(splits[17], part), 71), part)
    query_cotangent = draw_query_cotangent(jax.random.fold_in(jax.random.fold_in(splits[17], part), 71), part)
    output_cotangent = draw_output_cotangent(jax.random.fold_in(jax.random.fold_in(splits[17], part), 71), part)
    completion = jnp.searchsorted(jnp.cumsum(ragged_sizes(own_keys[4], COMP, TOKENS, MAXSEG, 0)), jnp.arange(TOKENS), side="right").astype(jnp.int32)
    rewards = jnp.clip(jax.random.uniform(own_keys[5], (COMP,), jnp.float32, 0.0, 1.0), 0.0, 1.0)
    query_down = scatter_about(own_keys[6], (D, RANK), D ** -0.5, 0.0625, ((0, 8),), jnp.float32)
    query_up = scatter_about(own_keys[7], (RANK, DQ), 0.03, 0.1875, ((1, 8),), jnp.float32)
    output_down = scatter_about(own_keys[8], (DQ, RANK), DQ ** -0.5, 0.0625, ((0, 8),), jnp.float32)
    output_up = scatter_about(own_keys[9], (RANK, D), 0.03, 0.1875, ((1, 8),), jnp.float32)
    query_fixed_weight = scatter_about(splits[10], (D, DQ), D ** -0.5, 0.0625, ((0, 2), (1, 8)))
    output_fixed_weight = noise_with(splits[11], (DQ, D), DQ ** -0.5, 0.09375, ((0, 8), (1, 2)), (0, 1, 8, 2.0))
    keyval_frozen = scatter_about(splits[12], (D, 2 * KVH * HD), D ** -0.5, 0.0625, ((0, 8),))
    decode_states = scatter_about(own_keys[13], (STEPS, ROWS, D), 1.0, 6.0, ((1, 2), (2, 8)))
    key_cache = draw_key_cache(jax.random.fold_in(jax.random.fold_in(splits[17], part), 71), part)
    value_cache = scatter_about(own_keys[15], (ROWS, KVH, CACHE, HD), 1.0, 6.0, ((0, 16),))
    cache_lengths = draw_cache_lengths(jax.random.fold_in(jax.random.fold_in(splits[17], part), 71), part)
    return dict(query_inputs=query_inputs, output_inputs=output_inputs, query_cotangent=query_cotangent, output_cotangent=output_cotangent, completion=completion, rewards=rewards, query_down=query_down, query_up=query_up, output_down=output_down, output_up=output_up, query_fixed_weight=query_fixed_weight, output_fixed_weight=output_fixed_weight, keyval_frozen=keyval_frozen, decode_states=decode_states, key_cache=key_cache, value_cache=value_cache, cache_lengths=cache_lengths)


adapter_scale_factor = 2.0
learn_rate = 8.0
clip_norm = 1.0

def attend(queries, cache_keys, cache_values, new_keys, new_values, valid_lengths, decode_step):
    score_scale = 1.0 / math.sqrt(queries.shape[-1])
    queries, new_keys, new_values = lax.optimization_barrier((queries, new_keys, new_values))
    query_wide = queries.astype(jnp.float32)
    s_cache = jnp.einsum('bgmd,bgcd->bgmc', query_wide, cache_keys.astype(jnp.float32)) * score_scale
    s_new = jnp.einsum('bgmd,bsgd->bgms', query_wide, new_keys.astype(jnp.float32)) * score_scale
    cache_ok = (jnp.arange(cache_keys.shape[2], dtype=jnp.int32)[None, :] < valid_lengths[:, None])[:, None, None, :]
    new_ok = (jnp.arange(new_keys.shape[1], dtype=jnp.int32) <= decode_step)[None, None, None, :]
    s_cache = jnp.where(cache_ok, s_cache, -jnp.inf)
    s_new = jnp.where(new_ok, s_new, -jnp.inf)
    highest = jnp.maximum(lax.optimization_barrier(jnp.max(s_cache, axis=-1)), lax.optimization_barrier(jnp.max(s_new, axis=-1)))[..., None]
    e_cache = jnp.exp(s_cache - highest)
    e_new = jnp.exp(s_new - highest)
    denominator = lax.optimization_barrier(jnp.sum(e_cache, axis=-1, keepdims=True)) + lax.optimization_barrier(jnp.sum(e_new, axis=-1, keepdims=True))
    p_cache = (e_cache / denominator).astype(jnp.bfloat16)
    p_new = (e_new / denominator).astype(jnp.bfloat16)
    p_cache, p_new = lax.optimization_barrier((p_cache, p_new))
    result = jnp.einsum('bgmc,bgcd->bgmd', p_cache.astype(jnp.float32), cache_values.astype(jnp.float32))
    result = result + jnp.einsum('bgms,bsgd->bgmd', p_new.astype(jnp.float32), new_values.astype(jnp.float32))
    return result.astype(jnp.bfloat16)

def weighted(token_weight, values_in):
    return (token_weight[:, None] * values_in).astype(jnp.bfloat16)

def reference(query_inputs, output_inputs, query_cotangent, output_cotangent, completion, rewards, query_down, query_up, output_down, output_up, query_fixed_weight, output_fixed_weight, keyval_frozen, decode_states, key_cache, value_cache, cache_lengths):
    advantage = rewards - jnp.mean(rewards)
    labels = jnp.arange(COMP, dtype=jnp.int32)
    token_weight = lax.optimization_barrier(jnp.sum(jnp.where(completion[:, None] == labels[None, :], advantage[None, :], 0.0), axis=1))
    down_q = query_down.astype(jnp.bfloat16)
    up_q = query_up.astype(jnp.bfloat16)
    down_o = output_down.astype(jnp.bfloat16)
    up_o = output_up.astype(jnp.bfloat16)
    inner_query = jnp.dot(query_inputs, down_q, preferred_element_type=jnp.float32)
    back_query = jnp.dot(query_cotangent, up_q.T, preferred_element_type=jnp.float32)
    inner_output = jnp.dot(output_inputs, down_o, preferred_element_type=jnp.float32)
    back_output = jnp.dot(output_cotangent, up_o.T, preferred_element_type=jnp.float32)
    grad_query_down = jnp.dot(query_inputs.T, weighted(token_weight, back_query), preferred_element_type=jnp.float32)
    grad_query_up = jnp.dot(weighted(token_weight, inner_query).T, query_cotangent, preferred_element_type=jnp.float32)
    grad_output_down = jnp.dot(output_inputs.T, weighted(token_weight, back_output), preferred_element_type=jnp.float32)
    grad_output_up = jnp.dot(weighted(token_weight, inner_output).T, output_cotangent, preferred_element_type=jnp.float32)
    total_sq = jnp.sum(grad_query_down * grad_query_down) + jnp.sum(grad_query_up * grad_query_up) + jnp.sum(grad_output_down * grad_output_down) + jnp.sum(grad_output_up * grad_output_up)
    shrink = clip_norm / (jnp.sqrt(total_sq) + 1e-06)
    new_query_down = query_down - learn_rate * shrink * grad_query_down
    new_query_up = query_up - learn_rate * shrink * grad_query_up
    new_output_down = output_down - learn_rate * shrink * grad_output_down
    new_output_up = output_up - learn_rate * shrink * grad_output_up
    query_down_norm = new_query_down.astype(jnp.bfloat16)
    query_up_norm = new_query_up.astype(jnp.bfloat16)
    output_down_norm = new_output_down.astype(jnp.bfloat16)
    output_up_norm = new_output_up.astype(jnp.bfloat16)
    query_combined_weight = (query_fixed_weight.astype(jnp.float32) + adapter_scale_factor * jnp.dot(query_down_norm, query_up_norm, preferred_element_type=jnp.float32)).astype(jnp.bfloat16)
    output_combined_weight = (output_fixed_weight.astype(jnp.float32) + adapter_scale_factor * jnp.dot(output_down_norm, output_up_norm, preferred_element_type=jnp.float32)).astype(jnp.bfloat16)
    group_heads = HEADS // KVH
    flattened = decode_states.reshape(STEPS * ROWS, D)
    queries = jnp.dot(flattened, query_combined_weight, preferred_element_type=jnp.float32).astype(jnp.bfloat16)
    queries = queries.reshape(STEPS, ROWS, KVH, group_heads, HD)
    new_entries = jnp.dot(flattened, keyval_frozen, preferred_element_type=jnp.float32).astype(jnp.bfloat16)
    new_entries = new_entries.reshape(STEPS, ROWS, 2, KVH, HD)
    new_keys = jnp.transpose(new_entries[:, :, 0], (1, 0, 2, 3))
    new_values = jnp.transpose(new_entries[:, :, 1], (1, 0, 2, 3))
    results = [attend(queries[decode_step], key_cache, value_cache, new_keys, new_values, cache_lengths, decode_step) for decode_step in range(STEPS)]
    attended = jnp.stack(results).reshape(STEPS * ROWS, N_TP, DQ // N_TP)
    head_blocks = jnp.transpose(attended, (1, 0, 2))
    weight_blocks = output_combined_weight.reshape(N_TP, DQ // N_TP, D)

    def add_block(carried, block_pair):
        partial_out = jnp.dot(block_pair[0], block_pair[1], preferred_element_type=jnp.float32).astype(jnp.bfloat16)
        partial_out = lax.optimization_barrier(partial_out)
        return (carried + partial_out.astype(jnp.float32), None)
    summed_out, _ = lax.scan(add_block, jnp.zeros((STEPS * ROWS, D), jnp.float32), (head_blocks, weight_blocks))
    decoded = summed_out.astype(jnp.bfloat16).reshape(STEPS, ROWS, D)
    return (decoded, new_query_down, new_query_up, new_output_down, new_output_up)
```

```python
import math

import jax
import jax.numpy as jnp
from jax import lax
from jax.experimental import pallas as pl
from jax.experimental.pallas import tpu as pltpu
from jax.sharding import PartitionSpec as P

HEADS = 64
KVH = 8
HD = 128


adapter_scale_factor = 2.0
learn_rate = 8.0
clip_norm = 1.0


def attend(queries, cache_keys, cache_values, new_keys, new_values, valid_lengths, decode_step):
    score_scale = 1.0 / math.sqrt(queries.shape[-1])
    s_cache = (
        jnp.einsum("bgmd,bgcd->bgmc", queries, cache_keys, preferred_element_type=jnp.float32)
        * score_scale
    )
    s_new = (
        jnp.einsum("bgmd,bsgd->bgms", queries, new_keys, preferred_element_type=jnp.float32)
        * score_scale
    )
    cache_ok = (jnp.arange(cache_keys.shape[2], dtype=jnp.int32)[None, :] < valid_lengths[:, None])[
        :, None, None, :
    ]
    new_ok = (jnp.arange(new_keys.shape[1], dtype=jnp.int32) <= decode_step)[None, None, None, :]
    s_cache = jnp.where(cache_ok, s_cache, -jnp.inf)
    s_new = jnp.where(new_ok, s_new, -jnp.inf)
    highest = jnp.maximum(jnp.max(s_cache, axis=-1), jnp.max(s_new, axis=-1))[..., None]
    e_cache = jnp.exp(s_cache - highest)
    e_new = jnp.exp(s_new - highest)
    denominator = jnp.sum(e_cache, axis=-1, keepdims=True) + jnp.sum(e_new, axis=-1, keepdims=True)
    p_cache = (e_cache / denominator).astype(jnp.bfloat16)
    p_new = (e_new / denominator).astype(jnp.bfloat16)
    result = jnp.einsum(
        "bgmc,bgcd->bgmd", p_cache, cache_values, preferred_element_type=jnp.float32
    )
    result = result + jnp.einsum(
        "bgms,bsgd->bgmd", p_new, new_values, preferred_element_type=jnp.float32
    )
    return result.astype(jnp.bfloat16)


def weighted(token_weight, values_in):
    return (token_weight[:, None] * values_in).astype(jnp.bfloat16)


def across(left, right):
    return lax.dot_general(
        left, right, (((0,), (0,)), ((), ())), preferred_element_type=jnp.float32
    )


def against(left, right):
    return lax.dot_general(
        left, right, (((1,), (1,)), ((), ())), preferred_element_type=jnp.float32
    )


def squares(gradients):
    return sum((jnp.sum(gradient * gradient) for gradient in gradients))


def on_device(
    query_inputs,
    output_inputs,
    query_cotangent,
    output_cotangent,
    completion,
    rewards,
    query_down,
    query_up,
    output_down,
    output_up,
    query_fixed_weight,
    output_fixed_weight,
    keyval_frozen,
    decode_states,
    key_cache,
    value_cache,
    cache_lengths,
):
    advantage = rewards - jnp.mean(rewards)
    labels = jnp.arange(rewards.shape[0], dtype=jnp.int32)
    token_weight = jnp.sum(
        jnp.where(completion[:, None] == labels[None, :], advantage[None, :], 0.0), axis=1
    )
    down_q = query_down.astype(jnp.bfloat16)
    up_q = query_up.astype(jnp.bfloat16)
    down_o = output_down.astype(jnp.bfloat16)
    up_o = output_up.astype(jnp.bfloat16)
    partials = (
        jnp.dot(query_inputs, down_q, preferred_element_type=jnp.float32),
        against(query_cotangent, up_q),
        jnp.dot(output_inputs, down_o, preferred_element_type=jnp.float32),
        against(output_cotangent, up_o),
    )
    inner_query, back_query, inner_output, back_output = (
        lax.psum(partials[0].astype(jnp.bfloat16), "tp").astype(jnp.float32),
        lax.psum(partials[1].astype(jnp.bfloat16), "tp").astype(jnp.float32),
        lax.psum(partials[2].astype(jnp.bfloat16), "tp").astype(jnp.float32),
        lax.psum(partials[3].astype(jnp.bfloat16), "tp").astype(jnp.float32),
    )
    terms = (
        across(query_inputs, weighted(token_weight, back_query)),
        across(query_cotangent, weighted(token_weight, inner_query)),
        across(output_inputs, weighted(token_weight, back_output)),
        across(output_cotangent, weighted(token_weight, inner_output)),
    )
    current = (query_down, query_up.T, output_down, output_up.T)
    gradients = (
        lax.psum(terms[0].astype(jnp.bfloat16), "dp").astype(jnp.float32),
        lax.psum(terms[1].astype(jnp.bfloat16), "dp").astype(jnp.float32),
        lax.psum(terms[2].astype(jnp.bfloat16), "dp").astype(jnp.float32),
        lax.psum(terms[3].astype(jnp.bfloat16), "dp").astype(jnp.float32),
    )
    total_sq = lax.psum(squares(gradients), "tp")
    shrink = clip_norm / (jnp.sqrt(total_sq) + 1e-06)
    updated = tuple(
        (
            factor_state - learn_rate * shrink * gradient
            for factor_state, gradient in zip(current, gradients)
        )
    )
    new_query_down = updated[0]
    new_query_up = updated[1].T
    new_output_down = updated[2]
    new_output_up = updated[3].T
    rollout_down_q = new_query_down.astype(jnp.bfloat16)
    rollout_up_q = new_query_up.astype(jnp.bfloat16)
    rollout_down_o = new_output_down.astype(jnp.bfloat16)
    rollout_up_o = new_output_up.astype(jnp.bfloat16)
    full_down_q, full_up_o = (
        lax.all_gather(rollout_down_q, "tp", axis=0, tiled=True),
        lax.all_gather(rollout_up_o, "tp", axis=1, tiled=True),
    )
    steps_count, row_count, local_width = decode_states.shape
    query_width = query_fixed_weight.shape[1]
    tp_count = lax.axis_size("tp")
    tp_rank = lax.axis_index("tp")
    adapter_weight_delta = jnp.dot(full_down_q, rollout_up_q, preferred_element_type=jnp.float32)
    query_combined_weight = (
        lax.all_gather(query_fixed_weight, "dp", axis=0, tiled=True).astype(jnp.float32)
        + adapter_scale_factor * adapter_weight_delta
    ).astype(jnp.bfloat16)
    adapter_weight_delta = jnp.dot(rollout_down_o, full_up_o, preferred_element_type=jnp.float32)
    output_combined_weight = (
        lax.all_gather(output_fixed_weight, "dp", axis=1, tiled=True).astype(jnp.float32)
        + adapter_scale_factor * adapter_weight_delta
    ).astype(jnp.bfloat16)
    queries = jnp.einsum(
        "srd,dh->srh",
        lax.all_gather(decode_states, "tp", axis=2, tiled=True),
        query_combined_weight,
        preferred_element_type=jnp.float32,
    ).astype(jnp.bfloat16)
    fresh_part = jnp.einsum(
        "srd,dk->srk", decode_states, keyval_frozen, preferred_element_type=jnp.float32
    )
    part_heads = query_width // HD
    group_heads = HEADS // KVH
    new_entries = lax.psum(fresh_part.astype(jnp.bfloat16), "tp")
    kv_head = tp_rank * part_heads // group_heads
    own_keys = lax.dynamic_slice_in_dim(new_entries, kv_head * HD, HD, 2)
    own_values = lax.dynamic_slice_in_dim(new_entries, (KVH + kv_head) * HD, HD, 2)
    copies = tp_count // KVH
    spread_keys = jnp.repeat(key_cache, copies, axis=1)
    spread_values = jnp.repeat(value_cache, copies, axis=1)
    head_keys, head_values = (
        lax.all_to_all(spread_keys, "tp", split_axis=1, concat_axis=0, tiled=True),
        lax.all_to_all(spread_values, "tp", split_axis=1, concat_axis=0, tiled=True),
    )
    query_heads = queries.reshape(steps_count, row_count, 1, part_heads, HD)
    step_keys = jnp.transpose(own_keys, (1, 0, 2))[:, :, None, :]
    step_values = jnp.transpose(own_values, (1, 0, 2))[:, :, None, :]
    results = [
        attend(
            query_heads[decode_step],
            head_keys,
            head_values,
            step_keys,
            step_values,
            cache_lengths,
            decode_step,
        )
        for decode_step in range(steps_count)
    ]
    attended = jnp.stack(results).reshape(steps_count, row_count, query_width)
    flattened = attended.reshape(steps_count * row_count, query_width)
    local_columns = output_combined_weight.shape[1] // tp_count
    summed_out = lax.psum_scatter(
        lax.dot_general(
            output_combined_weight,
            flattened,
            (((0,), (1,)), ((), ())),
            preferred_element_type=jnp.float32,
        ).astype(jnp.bfloat16),
        "tp",
        scatter_dimension=0,
        tiled=True,
    ).astype(jnp.float32)
    decoded = summed_out.T.reshape(steps_count, row_count, local_columns).astype(jnp.bfloat16)
    return (decoded, new_query_down, new_query_up, new_output_down, new_output_up)


MESH = pl.DeviceIdType.MESH
RANK = 64
LANES = 128
COLS = 256


def dot_nn(left, right):
    return jnp.dot(left, right, preferred_element_type=jnp.float32)


def landed(ref, sem):
    pltpu.make_async_copy(ref, ref, sem).wait()


def fused_kernel(
    n,
    xq,
    cq,
    xo,
    co,
    wq_hbm,
    wo_hbm,
    kv_hbm,
    states,
    kc,
    vc,
    token_weight,
    bias,
    qd,
    qu,
    od,
    ou,
    dec,
    new_qd,
    new_qu,
    new_od,
    new_ou,
    act,
    wq,
    wo,
    kv,
    factors,
    part,
    rs,
    own_w,
    wfull,
    gs,
    gr,
    gsum,
    kall,
    vall,
    ne_src,
    ne_recv,
    stf,
    small,
    small_recv,
    qp,
    qr,
    attall,
    al,
    al_recv,
    osrc,
    orecv,
    load_sem,
    kv_send,
    kv_recv,
    rs_send,
    rs_recv,
    ag_send,
    ag_recv,
    ne_sems,
    st_sems,
    g_send,
    g_recv,
    small_sems,
    q_sems,
    att_sems,
    al_sems,
    o_sems,
):
    d = lax.axis_index("dp")
    t = lax.axis_index("tp")
    other = 1 - d
    half = n // 2
    width = act.shape[2]
    rows = states.shape[0]
    cache = kc.shape[1]
    peers = [lax.rem(t + k, n) for k in range(n)]

    def load(source, target, index):
        pltpu.make_async_copy(source, target, load_sem.at[index]).start()

    def send(source, target, send_sem, recv_sem, device):
        pltpu.make_async_remote_copy(
            src_ref=source,
            dst_ref=target,
            send_sem=send_sem,
            recv_sem=recv_sem,
            device_id=device,
            device_id_type=MESH,
        ).start()

    for index, source in enumerate((xq, cq, xo, co)):
        load(source, act.at[index], index)
    load(kv_hbm, kv, 4)

    barrier = pltpu.get_barrier_semaphore()
    for k in range(n):
        if k > 0:
            pl.semaphore_signal(barrier, inc=1, device_id={"tp": peers[k]}, device_id_type=MESH)
        pl.semaphore_signal(
            barrier, inc=1, device_id={"dp": other, "tp": peers[k]}, device_id_type=MESH
        )

    factors[0] = qd[...].T.astype(jnp.bfloat16)
    factors[1] = qu[...].astype(jnp.bfloat16)
    factors[2] = od[...].T.astype(jnp.bfloat16)
    factors[3] = ou[...].astype(jnp.bfloat16)

    pl.semaphore_wait(barrier, 2 * n - 1)

    own_cache = pl.ds(pl.multiple_of(t * cache, cache), cache)
    for k in range(1, n):
        send(kc.at[peers[k]], kall.at[own_cache], kv_send.at[0], kv_recv.at[0], {"tp": peers[k]})
        send(vc.at[peers[k]], vall.at[own_cache], kv_send.at[1], kv_recv.at[1], {"tp": peers[k]})
    kall[own_cache, :] = kc[t]
    vall[own_cache, :] = vc[t]

    def project(m, carry):
        landed(act.at[m], load_sem.at[m])
        for c in range(width // COLS):
            block = against(factors[m], act[m, c * COLS : (c + 1) * COLS, :]).astype(jnp.bfloat16)
            for i in range(COLS // LANES):
                part[m, c * (COLS // LANES) + i] = block[:, i * LANES : (i + 1) * LANES]
        for k in range(1, n):
            send(
                part.at[m, peers[k]],
                rs.at[m, k - 1],
                rs_send.at[m],
                rs_recv.at[m],
                {"tp": peers[k]},
            )
        return carry

    lax.fori_loop(0, 4, project, 0)

    load(wq_hbm, wq, 5)
    load(wo_hbm, wo, 6)

    landed(kv, load_sem.at[4])
    for c in range(2 * n * HD // COLS):
        block = dot_nn(states[...], kv[:, c * COLS : (c + 1) * COLS]).astype(jnp.bfloat16)
        for i in range(COLS // HD):
            head = c * (COLS // HD) + i
            ne_src[head % n, head // n] = block[:, i * HD : (i + 1) * HD]

    own_tokens = pl.ds(pl.multiple_of(t * LANES, LANES), LANES)

    def reduce_weight(m, carry):
        landed(rs.at[m], rs_recv.at[m])
        total = part[m, t].astype(jnp.float32)
        for k in range(n - 1):
            total = total + rs[m, k].astype(jnp.float32)
        block = (total * token_weight[t]).astype(jnp.bfloat16)
        own_w[m] = block
        wfull[m, :, own_tokens] = block
        for k in range(1, n):
            send(
                own_w.at[m],
                wfull.at[m, :, own_tokens],
                ag_send.at[m],
                ag_recv.at[m],
                {"tp": peers[k]},
            )
        return carry

    lax.fori_loop(0, 4, reduce_weight, 0)

    for k in range(1, n):
        send(ne_src.at[peers[k]], ne_recv.at[k - 1], ne_sems.at[0], ne_sems.at[1], {"tp": peers[k]})

    home = lax.div(t, half)
    stays = home == d
    st_place = stf.at[lax.rem(t, half), pl.ds(pl.multiple_of(d * rows, rows), rows)]
    for k in range(1, n):
        send(states, st_place, st_sems.at[0], st_sems.at[1], {"dp": home, "tp": peers[k]})

    @pl.when(stays)
    def _():
        pltpu.make_async_copy(states, st_place, st_sems.at[1]).start()

    @pl.when(jnp.logical_not(stays))
    def _():
        send(states, st_place, st_sems.at[0], st_sems.at[1], {"dp": other})

    others = pl.ds(0, (n - 1) * LANES)

    def gradient(i, carry):
        m = i + 1 - 2 * lax.rem(i, 2)
        landed(wfull.at[i, :, others], ag_recv.at[i])
        for c in range(width // COLS):
            at = slice(c * COLS, (c + 1) * COLS)
            gs[m, :, at] = dot_nn(wfull[i], act[m, :, at]).astype(jnp.bfloat16)
        send(gs.at[m], gr.at[m], g_send.at[m], g_recv.at[m], {"dp": other})
        return carry

    lax.fori_loop(0, 4, gradient, 0)

    squared = jnp.zeros((8, LANES), jnp.float32)
    for m in (1, 0, 3, 2):
        landed(gr.at[m], g_recv.at[m])
        total = gs[m].astype(jnp.float32) + gr[m].astype(jnp.float32)
        gsum[m] = total
        square = total * total
        for a in range(RANK // 8):
            for b in range(width // LANES):
                squared = squared + square[a * 8 : (a + 1) * 8, b * LANES : (b + 1) * LANES]
    small[:rows, :RANK] = against(states[...], gsum[0].astype(jnp.bfloat16))
    small[:rows, RANK:] = against(states[...], factors[0])
    small[rows:, :] = squared
    for k in range(1, n):
        send(small, small_recv.at[k - 1], small_sems.at[0], small_sems.at[1], {"tp": peers[k]})

    landed(stf, st_sems.at[1])
    landed(wq, load_sem.at[5])

    def queries(c, carry):
        at = pl.ds(pl.multiple_of(c * COLS, COLS), COLS)
        total = dot_nn(stf[0], wq[0:width, at])
        for j in range(1, half):
            total = total + dot_nn(stf[j], wq[j * width : (j + 1) * width, at])
        qp[0, :, at] = total[:rows]
        qp[1, :, at] = total[rows:]
        return carry

    lax.fori_loop(0, width // COLS, queries, 0)
    send(qp.at[other], qr, q_sems.at[0], q_sems.at[1], {"dp": other})

    landed(ne_recv, ne_sems.at[1])
    fresh = ne_src[t].astype(jnp.float32)
    for k in range(n - 1):
        fresh = fresh + ne_recv[k].astype(jnp.float32)
    fresh = fresh.astype(jnp.bfloat16)

    landed(small_recv, small_sems.at[1])
    total = small[...]
    for k in range(n - 1):
        total = total + small_recv[k]
    norm = jnp.sqrt(jnp.sum(total[rows:, :], axis=(0, 1), keepdims=True))
    step = learn_rate * (clip_norm / (norm + 1e-06))
    new_up_q = qu[...] - step * gsum[1]
    new_qu[...] = new_up_q
    inner = (total[:rows, RANK:] - step * total[:rows, :RANK]).astype(jnp.bfloat16)
    lora = dot_nn(inner, new_up_q.astype(jnp.bfloat16))

    landed(qr, q_sems.at[1])
    query = (qp[d] + qr[...] + adapter_scale_factor * lora).astype(jnp.bfloat16)
    heads = width // HD
    stacked = jnp.concatenate([query[:, h * HD : (h + 1) * HD] for h in range(heads)], axis=0)

    landed(kall.at[pl.ds(0, (n - 1) * cache)], kv_recv.at[0])
    landed(vall.at[pl.ds(0, (n - 1) * cache)], kv_recv.at[1])
    count = rows * heads
    scale = 1.0 / math.sqrt(HD)
    low = jnp.float32(-1e30)
    s_old = against(stacked, kall[...]) * scale + bias[...]
    s_new = against(stacked, fresh[0]) * scale
    row_old = lax.broadcasted_iota(jnp.int32, s_old.shape, 0)
    col_old = lax.broadcasted_iota(jnp.int32, s_old.shape, 1)
    s_old = jnp.where(jnp.bitwise_and(row_old, n - 1) == lax.div(col_old, cache), s_old, low)
    row_new = lax.broadcasted_iota(jnp.int32, s_new.shape, 0)
    col_new = lax.broadcasted_iota(jnp.int32, s_new.shape, 1)
    same = jnp.bitwise_and(row_new, n - 1) == jnp.bitwise_and(col_new, n - 1)
    known = col_new <= jnp.bitwise_and(row_new, rows - 1)
    s_new = jnp.where(jnp.logical_and(same, known), s_new, low)
    highest = jnp.maximum(
        jnp.max(s_old, axis=1, keepdims=True), jnp.max(s_new, axis=1, keepdims=True)
    )
    e_old = jnp.exp(s_old - highest)
    e_new = jnp.exp(s_new - highest)
    denominator = jnp.sum(e_old, axis=1, keepdims=True) + jnp.sum(e_new, axis=1, keepdims=True)
    result = dot_nn((e_old / denominator).astype(jnp.bfloat16), vall[...])
    result = result + dot_nn((e_new / denominator).astype(jnp.bfloat16), fresh[1])
    result = result.astype(jnp.bfloat16)
    attended = jnp.concatenate(
        [result[h * rows : (h + 1) * rows, :] for h in range(heads)], axis=1
    )
    attall[d] = attended
    send(attall.at[d], attall.at[d], att_sems.at[0], att_sems.at[1], {"dp": other})

    down_step = step * gsum[2]
    new_down_o = od[...].T - down_step
    al[:, :RANK] = against(attended, new_down_o.astype(jnp.bfloat16))
    al[:, RANK:] = jnp.zeros((rows, LANES - RANK), jnp.float32)
    for k in range(1, n):
        send(al, al_recv.at[k - 1], al_sems.at[0], al_sems.at[1], {"tp": peers[k]})

    landed(wo, load_sem.at[6])
    landed(attall.at[other], att_sems.at[1])
    both = attall[...].reshape(2 * rows, width)

    def outputs(j, carry):
        for c in range(width // COLS):
            at = pl.ds(pl.multiple_of(j * width + c * COLS, COLS), COLS)
            block = dot_nn(both, wo[:, at]).astype(jnp.bfloat16)
            osrc[j, 0, :, c * COLS : (c + 1) * COLS] = block[:rows]
            osrc[j, 1, :, c * COLS : (c + 1) * COLS] = block[rows:]
        owner = half * d + j
        send(
            osrc.at[j, other],
            orecv.at[t],
            o_sems.at[0],
            o_sems.at[1],
            {"dp": other, "tp": owner},
        )
        mine = owner == t

        @pl.when(mine)
        def _():
            pltpu.make_async_copy(osrc.at[j, d], orecv.at[t], o_sems.at[1]).start()

        @pl.when(jnp.logical_not(mine))
        def _():
            send(osrc.at[j, d], orecv.at[t], o_sems.at[0], o_sems.at[1], {"tp": owner})

        return carry

    lax.fori_loop(0, half, outputs, 0)

    new_up_o = ou[...] - step * gsum[3]
    new_ou[...] = new_up_o
    new_od[...] = new_down_o.T
    new_qd[...] = qd[...] - (step * gsum[0]).T

    landed(al_recv, al_sems.at[1])
    inner = al[...]
    for k in range(n - 1):
        inner = inner + al_recv[k]
    lora = dot_nn(inner[:, :RANK].astype(jnp.bfloat16), new_up_o.astype(jnp.bfloat16))

    landed(orecv, o_sems.at[1])
    total = adapter_scale_factor * lora
    for k in range(n):
        total = total + orecv[k].astype(jnp.float32)
    dec[...] = total.astype(jnp.bfloat16)

    landed(kall.at[pl.ds(0, (n - 1) * cache)], kv_send.at[0])
    landed(vall.at[pl.ds(0, (n - 1) * cache)], kv_send.at[1])
    for m in range(4):
        landed(rs.at[m], rs_send.at[m])
        landed(wfull.at[m, :, others], ag_send.at[m])
        landed(gs.at[m], g_send.at[m])
    landed(ne_recv, ne_sems.at[0])
    landed(small_recv, small_sems.at[0])
    landed(qr, q_sems.at[0])
    landed(attall.at[d], att_sems.at[0])
    landed(al_recv, al_sems.at[0])
    landed(orecv.at[pl.ds(0, n - 1)], o_sems.at[0])
    for k in range(n - 1):
        landed(states, st_sems.at[0])

    @pl.when(jnp.logical_not(stays))
    def _():
        landed(states, st_sems.at[0])
        landed(orecv.at[0], o_sems.at[0])


def fused(
    query_inputs,
    output_inputs,
    query_cotangent,
    output_cotangent,
    completion,
    rewards,
    query_down,
    query_up,
    output_down,
    output_up,
    query_fixed_weight,
    output_fixed_weight,
    keyval_frozen,
    decode_states,
    key_cache,
    value_cache,
    cache_lengths,
):
    n = lax.axis_size("tp")
    tokens, width = query_inputs.shape
    steps_count, row_count, _ = decode_states.shape
    rows = steps_count * row_count
    cache = key_cache.shape[2]
    advantage = rewards - jnp.mean(rewards)
    labels = jnp.arange(rewards.shape[0], dtype=jnp.int32)
    token_weight = jnp.sum(
        jnp.where(completion[:, None] == labels[None, :], advantage[None, :], 0.0), axis=1
    ).reshape(n, 1, tokens // n)
    valid = jnp.arange(cache, dtype=jnp.int32)[None, :] < cache_lengths[:, None]
    bias = jnp.where(valid, 0.0, -1e30).astype(jnp.float32).reshape(1, row_count * cache)
    vmem = pl.BlockSpec(memory_space=pltpu.VMEM)
    hbm = pl.BlockSpec(memory_space=pl.ANY)
    bf16, f32 = jnp.bfloat16, jnp.float32
    dma = pltpu.SemaphoreType.DMA
    outs = pl.pallas_call(
        lambda *refs: fused_kernel(n, *refs),
        out_shape=(
            jax.ShapeDtypeStruct((rows, width), bf16),
            jax.ShapeDtypeStruct(query_down.shape, f32),
            jax.ShapeDtypeStruct(query_up.shape, f32),
            jax.ShapeDtypeStruct(output_down.shape, f32),
            jax.ShapeDtypeStruct(output_up.shape, f32),
        ),
        in_specs=[hbm] * 7 + [vmem] * 9,
        out_specs=(vmem,) * 5,
        scratch_shapes=[
            pltpu.VMEM((4, tokens, width), bf16),
            pltpu.VMEM(query_fixed_weight.shape, bf16),
            pltpu.VMEM(output_fixed_weight.shape, bf16),
            pltpu.VMEM(keyval_frozen.shape, bf16),
            pltpu.VMEM((4, RANK, width), bf16),
            pltpu.VMEM((4, n, RANK, LANES), bf16),
            pltpu.VMEM((4, n - 1, RANK, LANES), bf16),
            pltpu.VMEM((4, RANK, LANES), bf16),
            pltpu.VMEM((4, RANK, tokens), bf16),
            pltpu.VMEM((4, RANK, width), bf16),
            pltpu.VMEM((4, RANK, width), bf16),
            pltpu.VMEM((4, RANK, width), f32),
            pltpu.VMEM((n * cache, HD), bf16),
            pltpu.VMEM((n * cache, HD), bf16),
            pltpu.VMEM((n, 2, rows, HD), bf16),
            pltpu.VMEM((n - 1, 2, rows, HD), bf16),
            pltpu.VMEM((n // 2, 2 * rows, width), bf16),
            pltpu.VMEM((rows + 8, LANES), f32),
            pltpu.VMEM((n - 1, rows + 8, LANES), f32),
            pltpu.VMEM((2, rows, width), f32),
            pltpu.VMEM((rows, width), f32),
            pltpu.VMEM((2, rows, width), bf16),
            pltpu.VMEM((rows, LANES), f32),
            pltpu.VMEM((n - 1, rows, LANES), f32),
            pltpu.VMEM((n // 2, 2, rows, width), bf16),
            pltpu.VMEM((n, rows, width), bf16),
            dma((7,)),
            dma((2,)),
            dma((2,)),
            dma((4,)),
            dma((4,)),
            dma((4,)),
            dma((4,)),
            dma((2,)),
            dma((2,)),
            dma((4,)),
            dma((4,)),
            dma((2,)),
            dma((2,)),
            dma((2,)),
            dma((2,)),
            dma((2,)),
        ],
        compiler_params=pltpu.CompilerParams(
            collective_id=0, has_side_effects=True, vmem_limit_bytes=56 << 20
        ),
        cost_estimate=pl.CostEstimate(
            flops=4 * 10**9, bytes_accessed=36 * 10**6, transcendentals=1 << 17
        ),
    )(
        query_inputs,
        query_cotangent,
        output_inputs,
        output_cotangent,
        query_fixed_weight,
        output_fixed_weight,
        keyval_frozen,
        decode_states.reshape(rows, width),
        key_cache[0],
        value_cache[0],
        token_weight,
        bias,
        query_down,
        query_up,
        output_down,
        output_up,
    )
    decoded = outs[0].reshape(steps_count, row_count, width)
    return (decoded, *outs[1:])


def fits(mesh):
    return mesh.shape["dp"] == 2 and mesh.shape["tp"] == KVH


def solution(mesh):
    return jax.shard_map(
        fused if fits(mesh) else on_device,
        mesh=mesh,
        in_specs=(
            P(("grp", "dp"), "tp"),
            P(("grp", "dp"), "tp"),
            P(("grp", "dp"), "tp"),
            P(("grp", "dp"), "tp"),
            P(("grp", "dp")),
            P("grp"),
            P(("grp", "tp"), None),
            P("grp", "tp"),
            P(("grp", "tp"), None),
            P("grp", "tp"),
            P("dp", "tp"),
            P("tp", "dp"),
            P("tp", None),
            P(None, ("grp", "dp"), "tp"),
            P(("grp", "dp", "tp"), None, None, None),
            P(("grp", "dp", "tp"), None, None, None),
            P(("grp", "dp")),
        ),
        out_specs=(
            P(None, ("grp", "dp"), "tp"),
            P(("grp", "tp"), None),
            P("grp", "tp"),
            P(("grp", "tp"), None),
            P("grp", "tp"),
        ),
        check_vma=False,
    )
```

```python
import math

import jax
import jax.numpy as jnp
from jax import lax
from jax.experimental import pallas as pl
from jax.experimental.pallas import tpu as pltpu
from jax.sharding import PartitionSpec as P

HEADS = 64
KVH = 8
HD = 128


adapter_scale_factor = 2.0
learn_rate = 8.0
clip_norm = 1.0


def attend(queries, cache_keys, cache_values, new_keys, new_values, valid_lengths, decode_step):
    score_scale = 1.0 / math.sqrt(queries.shape[-1])
    s_cache = (
        jnp.einsum("bgmd,bgcd->bgmc", queries, cache_keys, preferred_element_type=jnp.float32)
        * score_scale
    )
    s_new = (
        jnp.einsum("bgmd,bsgd->bgms", queries, new_keys, preferred_element_type=jnp.float32)
        * score_scale
    )
    cache_ok = (jnp.arange(cache_keys.shape[2], dtype=jnp.int32)[None, :] < valid_lengths[:, None])[
        :, None, None, :
    ]
    new_ok = (jnp.arange(new_keys.shape[1], dtype=jnp.int32) <= decode_step)[None, None, None, :]
    s_cache = jnp.where(cache_ok, s_cache, -jnp.inf)
    s_new = jnp.where(new_ok, s_new, -jnp.inf)
    highest = jnp.maximum(jnp.max(s_cache, axis=-1), jnp.max(s_new, axis=-1))[..., None]
    e_cache = jnp.exp(s_cache - highest)
    e_new = jnp.exp(s_new - highest)
    denominator = jnp.sum(e_cache, axis=-1, keepdims=True) + jnp.sum(e_new, axis=-1, keepdims=True)
    p_cache = (e_cache / denominator).astype(jnp.bfloat16)
    p_new = (e_new / denominator).astype(jnp.bfloat16)
    result = jnp.einsum(
        "bgmc,bgcd->bgmd", p_cache, cache_values, preferred_element_type=jnp.float32
    )
    result = result + jnp.einsum(
        "bgms,bsgd->bgmd", p_new, new_values, preferred_element_type=jnp.float32
    )
    return result.astype(jnp.bfloat16)


def weighted(token_weight, values_in):
    return (token_weight[:, None] * values_in).astype(jnp.bfloat16)


def across(left, right):
    return lax.dot_general(
        left, right, (((0,), (0,)), ((), ())), preferred_element_type=jnp.float32
    )


def against(left, right):
    return lax.dot_general(
        left, right, (((1,), (1,)), ((), ())), preferred_element_type=jnp.float32
    )


def squares(gradients):
    return sum((jnp.sum(gradient * gradient) for gradient in gradients))


def on_device(
    query_inputs,
    output_inputs,
    query_cotangent,
    output_cotangent,
    completion,
    rewards,
    query_down,
    query_up,
    output_down,
    output_up,
    query_fixed_weight,
    output_fixed_weight,
    keyval_frozen,
    decode_states,
    key_cache,
    value_cache,
    cache_lengths,
):
    advantage = rewards - jnp.mean(rewards)
    labels = jnp.arange(rewards.shape[0], dtype=jnp.int32)
    token_weight = jnp.sum(
        jnp.where(completion[:, None] == labels[None, :], advantage[None, :], 0.0), axis=1
    )
    down_q = query_down.astype(jnp.bfloat16)
    up_q = query_up.astype(jnp.bfloat16)
    down_o = output_down.astype(jnp.bfloat16)
    up_o = output_up.astype(jnp.bfloat16)
    partials = (
        jnp.dot(query_inputs, down_q, preferred_element_type=jnp.float32),
        against(query_cotangent, up_q),
        jnp.dot(output_inputs, down_o, preferred_element_type=jnp.float32),
        against(output_cotangent, up_o),
    )
    inner_query, back_query, inner_output, back_output = (
        lax.psum(partials[0].astype(jnp.bfloat16), "tp").astype(jnp.float32),
        lax.psum(partials[1].astype(jnp.bfloat16), "tp").astype(jnp.float32),
        lax.psum(partials[2].astype(jnp.bfloat16), "tp").astype(jnp.float32),
        lax.psum(partials[3].astype(jnp.bfloat16), "tp").astype(jnp.float32),
    )
    terms = (
        across(query_inputs, weighted(token_weight, back_query)),
        across(query_cotangent, weighted(token_weight, inner_query)),
        across(output_inputs, weighted(token_weight, back_output)),
        across(output_cotangent, weighted(token_weight, inner_output)),
    )
    current = (query_down, query_up.T, output_down, output_up.T)
    gradients = (
        lax.psum(terms[0].astype(jnp.bfloat16), "dp").astype(jnp.float32),
        lax.psum(terms[1].astype(jnp.bfloat16), "dp").astype(jnp.float32),
        lax.psum(terms[2].astype(jnp.bfloat16), "dp").astype(jnp.float32),
        lax.psum(terms[3].astype(jnp.bfloat16), "dp").astype(jnp.float32),
    )
    total_sq = lax.psum(squares(gradients), "tp")
    shrink = clip_norm / (jnp.sqrt(total_sq) + 1e-06)
    updated = tuple(
        (
            factor_state - learn_rate * shrink * gradient
            for factor_state, gradient in zip(current, gradients)
        )
    )
    new_query_down = updated[0]
    new_query_up = updated[1].T
    new_output_down = updated[2]
    new_output_up = updated[3].T
    rollout_down_q = new_query_down.astype(jnp.bfloat16)
    rollout_up_q = new_query_up.astype(jnp.bfloat16)
    rollout_down_o = new_output_down.astype(jnp.bfloat16)
    rollout_up_o = new_output_up.astype(jnp.bfloat16)
    full_down_q, full_up_o = (
        lax.all_gather(rollout_down_q, "tp", axis=0, tiled=True),
        lax.all_gather(rollout_up_o, "tp", axis=1, tiled=True),
    )
    steps_count, row_count, local_width = decode_states.shape
    query_width = query_fixed_weight.shape[1]
    tp_count = lax.axis_size("tp")
    tp_rank = lax.axis_index("tp")
    adapter_weight_delta = jnp.dot(full_down_q, rollout_up_q, preferred_element_type=jnp.float32)
    query_combined_weight = (
        lax.all_gather(query_fixed_weight, "dp", axis=0, tiled=True).astype(jnp.float32)
        + adapter_scale_factor * adapter_weight_delta
    ).astype(jnp.bfloat16)
    adapter_weight_delta = jnp.dot(rollout_down_o, full_up_o, preferred_element_type=jnp.float32)
    output_combined_weight = (
        lax.all_gather(output_fixed_weight, "dp", axis=1, tiled=True).astype(jnp.float32)
        + adapter_scale_factor * adapter_weight_delta
    ).astype(jnp.bfloat16)
    queries = jnp.einsum(
        "srd,dh->srh",
        lax.all_gather(decode_states, "tp", axis=2, tiled=True),
        query_combined_weight,
        preferred_element_type=jnp.float32,
    ).astype(jnp.bfloat16)
    fresh_part = jnp.einsum(
        "srd,dk->srk", decode_states, keyval_frozen, preferred_element_type=jnp.float32
    )
    part_heads = query_width // HD
    group_heads = HEADS // KVH
    new_entries = lax.psum(fresh_part.astype(jnp.bfloat16), "tp")
    kv_head = tp_rank * part_heads // group_heads
    own_keys = lax.dynamic_slice_in_dim(new_entries, kv_head * HD, HD, 2)
    own_values = lax.dynamic_slice_in_dim(new_entries, (KVH + kv_head) * HD, HD, 2)
    copies = tp_count // KVH
    spread_keys = jnp.repeat(key_cache, copies, axis=1)
    spread_values = jnp.repeat(value_cache, copies, axis=1)
    head_keys, head_values = (
        lax.all_to_all(spread_keys, "tp", split_axis=1, concat_axis=0, tiled=True),
        lax.all_to_all(spread_values, "tp", split_axis=1, concat_axis=0, tiled=True),
    )
    query_heads = queries.reshape(steps_count, row_count, 1, part_heads, HD)
    step_keys = jnp.transpose(own_keys, (1, 0, 2))[:, :, None, :]
    step_values = jnp.transpose(own_values, (1, 0, 2))[:, :, None, :]
    results = [
        attend(
            query_heads[decode_step],
            head_keys,
            head_values,
            step_keys,
            step_values,
            cache_lengths,
            decode_step,
        )
        for decode_step in range(steps_count)
    ]
    attended = jnp.stack(results).reshape(steps_count, row_count, query_width)
    flattened = attended.reshape(steps_count * row_count, query_width)
    local_columns = output_combined_weight.shape[1] // tp_count
    summed_out = lax.psum_scatter(
        lax.dot_general(
            output_combined_weight,
            flattened,
            (((0,), (1,)), ((), ())),
            preferred_element_type=jnp.float32,
        ).astype(jnp.bfloat16),
        "tp",
        scatter_dimension=0,
        tiled=True,
    ).astype(jnp.float32)
    decoded = summed_out.T.reshape(steps_count, row_count, local_columns).astype(jnp.bfloat16)
    return (decoded, new_query_down, new_query_up, new_output_down, new_output_up)


MESH = pl.DeviceIdType.MESH
RANK = 64
LANES = 128
COLS = 256


def dot_nn(left, right):
    return jnp.dot(left, right, preferred_element_type=jnp.float32)


def landed(ref, sem):
    pltpu.make_async_copy(ref, ref, sem).wait()


def fused_kernel(
    n,
    xq,
    cq,
    xo,
    co,
    wq_hbm,
    wo_hbm,
    kv_hbm,
    states_hbm,
    kc,
    vc,
    completion,
    rewards,
    lengths,
    qd_hbm,
    qu_hbm,
    od_hbm,
    ou_hbm,
    dec_out,
    new_out,
    states,
    held,
    updated,
    dec,
    act,
    wq,
    wo,
    kv,
    factors,
    part,
    rs,
    own_w,
    wfull,
    gs,
    gr,
    gsum,
    kall,
    vall,
    ne_src,
    ne_recv,
    stf,
    small,
    small_recv,
    qp,
    qr,
    attall,
    al,
    al_recv,
    osrc,
    orecv,
    load_sem,
    kv_send,
    kv_recv,
    rs_send,
    rs_recv,
    ag_send,
    ag_recv,
    ne_sems,
    st_sems,
    g_send,
    g_recv,
    small_sems,
    q_sems,
    att_sems,
    al_sems,
    o_sems,
    out_sems,
):
    d = lax.axis_index("dp")
    t = lax.axis_index("tp")
    other = 1 - d
    half = n // 2
    width = act.shape[2]
    rows = states.shape[0]
    cache = kc.shape[1]
    peers = [lax.rem(t + k, n) for k in range(n)]

    def load(source, target, index):
        pltpu.make_async_copy(source, target, load_sem.at[index]).start()

    def send(source, target, send_sem, recv_sem, device):
        pltpu.make_async_remote_copy(
            src_ref=source,
            dst_ref=target,
            send_sem=send_sem,
            recv_sem=recv_sem,
            device_id=device,
            device_id_type=MESH,
        ).start()

    load(states_hbm, states, 7)
    for index, source in enumerate((qd_hbm, qu_hbm, od_hbm, ou_hbm)):
        load(source, held.at[index], 8 + index)
    for index, source in enumerate((xq, cq, xo, co)):
        load(source, act.at[index], index)
    load(kv_hbm, kv, 4)

    barrier = pltpu.get_barrier_semaphore()
    for k in range(n):
        if k > 0:
            pl.semaphore_signal(barrier, inc=1, device_id={"tp": peers[k]}, device_id_type=MESH)
        pl.semaphore_signal(
            barrier, inc=1, device_id={"dp": other, "tp": peers[k]}, device_id_type=MESH
        )

    for m in range(4):
        landed(held.at[m], load_sem.at[8 + m])
        factors[m] = held[m].astype(jnp.bfloat16)
    count = rewards.shape[0]
    mean = rewards[0]
    for c in range(1, count):
        mean = mean + rewards[c]
    mean = mean / count
    own_completion = completion[t]
    token_weight = jnp.zeros(own_completion.shape, jnp.float32)
    for c in range(count):
        token_weight = jnp.where(own_completion == c, rewards[c] - mean, token_weight)

    pl.semaphore_wait(barrier, 2 * n - 1)

    own_cache = pl.ds(pl.multiple_of(t * cache, cache), cache)
    for k in range(1, n):
        send(kc.at[peers[k]], kall.at[own_cache], kv_send.at[0], kv_recv.at[0], {"tp": peers[k]})
        send(vc.at[peers[k]], vall.at[own_cache], kv_send.at[1], kv_recv.at[1], {"tp": peers[k]})
    load(kc.at[t], kall.at[own_cache], 12)
    load(vc.at[t], vall.at[own_cache], 13)

    def project(m, carry):
        landed(act.at[m], load_sem.at[m])
        for c in range(width // COLS):
            block = against(factors[m], act[m, c * COLS : (c + 1) * COLS, :]).astype(jnp.bfloat16)
            for i in range(COLS // LANES):
                part[m, c * (COLS // LANES) + i] = block[:, i * LANES : (i + 1) * LANES]
        for k in range(1, n):
            send(
                part.at[m, peers[k]],
                rs.at[m, k - 1],
                rs_send.at[m],
                rs_recv.at[m],
                {"tp": peers[k]},
            )
        return carry

    lax.fori_loop(0, 4, project, 0)

    load(wq_hbm, wq, 5)
    load(wo_hbm, wo, 6)

    landed(states, load_sem.at[7])
    landed(kv, load_sem.at[4])
    for c in range(2 * n * HD // COLS):
        block = dot_nn(states[...], kv[:, c * COLS : (c + 1) * COLS]).astype(jnp.bfloat16)
        for i in range(COLS // HD):
            head = c * (COLS // HD) + i
            ne_src[head % n, head // n] = block[:, i * HD : (i + 1) * HD]

    own_tokens = pl.ds(pl.multiple_of(t * LANES, LANES), LANES)

    def reduce_weight(m, carry):
        landed(rs.at[m], rs_recv.at[m])
        total = part[m, t].astype(jnp.float32)
        for k in range(n - 1):
            total = total + rs[m, k].astype(jnp.float32)
        block = (total * token_weight).astype(jnp.bfloat16)
        own_w[m] = block
        wfull[m, :, own_tokens] = block
        for k in range(1, n):
            send(
                own_w.at[m],
                wfull.at[m, :, own_tokens],
                ag_send.at[m],
                ag_recv.at[m],
                {"tp": peers[k]},
            )
        return carry

    lax.fori_loop(0, 4, reduce_weight, 0)

    for k in range(1, n):
        send(ne_src.at[peers[k]], ne_recv.at[k - 1], ne_sems.at[0], ne_sems.at[1], {"tp": peers[k]})

    home = lax.div(t, half)
    stays = home == d
    st_place = stf.at[lax.rem(t, half), pl.ds(pl.multiple_of(d * rows, rows), rows)]
    for k in range(1, n):
        send(states, st_place, st_sems.at[0], st_sems.at[1], {"dp": home, "tp": peers[k]})

    @pl.when(stays)
    def _():
        pltpu.make_async_copy(states, st_place, st_sems.at[1]).start()

    @pl.when(jnp.logical_not(stays))
    def _():
        send(states, st_place, st_sems.at[0], st_sems.at[1], {"dp": other})

    others = pl.ds(0, (n - 1) * LANES)

    def gradient(i, carry):
        m = i + 1 - 2 * lax.rem(i, 2)
        landed(wfull.at[i, :, others], ag_recv.at[i])
        for c in range(width // COLS):
            at = slice(c * COLS, (c + 1) * COLS)
            gs[m, :, at] = dot_nn(wfull[i], act[m, :, at]).astype(jnp.bfloat16)
        send(gs.at[m], gr.at[m], g_send.at[m], g_recv.at[m], {"dp": other})
        return carry

    lax.fori_loop(0, 4, gradient, 0)

    squared = jnp.zeros((8, LANES), jnp.float32)
    for m in (1, 0, 3, 2):
        landed(gr.at[m], g_recv.at[m])
        total = gs[m].astype(jnp.float32) + gr[m].astype(jnp.float32)
        gsum[m] = total
        square = total * total
        for a in range(RANK // 8):
            for b in range(width // LANES):
                squared = squared + square[a * 8 : (a + 1) * 8, b * LANES : (b + 1) * LANES]
    small[:rows, :RANK] = against(states[...], gsum[0].astype(jnp.bfloat16))
    small[:rows, RANK:] = against(states[...], factors[0])
    small[rows:, :] = squared
    for k in range(1, n):
        send(small, small_recv.at[k - 1], small_sems.at[0], small_sems.at[1], {"tp": peers[k]})

    landed(stf, st_sems.at[1])
    landed(wq, load_sem.at[5])

    def queries(c, carry):
        at = pl.ds(pl.multiple_of(c * COLS, COLS), COLS)
        total = dot_nn(stf[0], wq[0:width, at])
        for j in range(1, half):
            total = total + dot_nn(stf[j], wq[j * width : (j + 1) * width, at])
        qp[0, :, at] = total[:rows]
        qp[1, :, at] = total[rows:]
        return carry

    lax.fori_loop(0, width // COLS, queries, 0)
    send(qp.at[other], qr, q_sems.at[0], q_sems.at[1], {"dp": other})

    landed(ne_recv, ne_sems.at[1])
    fresh = ne_src[t].astype(jnp.float32)
    for k in range(n - 1):
        fresh = fresh + ne_recv[k].astype(jnp.float32)
    fresh = fresh.astype(jnp.bfloat16)

    landed(small_recv, small_sems.at[1])
    total = small[...]
    for k in range(n - 1):
        total = total + small_recv[k]
    norm = jnp.sqrt(jnp.sum(total[rows:, :], axis=(0, 1), keepdims=True))
    step = learn_rate * (clip_norm / (norm + 1e-06))
    for m in range(4):
        updated[m] = held[m] - step * gsum[m]
        pltpu.make_async_copy(updated.at[m], new_out.at[m], out_sems.at[m]).start()
    inner = (total[:rows, RANK:] - step * total[:rows, :RANK]).astype(jnp.bfloat16)
    lora = dot_nn(inner, updated[1].astype(jnp.bfloat16))

    landed(qr, q_sems.at[1])
    query = (qp[d] + qr[...] + adapter_scale_factor * lora).astype(jnp.bfloat16)
    heads = width // HD
    stacked = jnp.concatenate([query[:, h * HD : (h + 1) * HD] for h in range(heads)], axis=0)

    landed(kall.at[own_cache], load_sem.at[12])
    landed(vall.at[own_cache], load_sem.at[13])
    landed(kall.at[pl.ds(0, (n - 1) * cache)], kv_recv.at[0])
    landed(vall.at[pl.ds(0, (n - 1) * cache)], kv_recv.at[1])
    scale = 1.0 / math.sqrt(HD)
    low = jnp.float32(-1e30)
    s_old = against(stacked, kall[...]) * scale
    s_new = against(stacked, fresh[0]) * scale
    row_old = lax.broadcasted_iota(jnp.int32, s_old.shape, 0)
    column = lax.broadcasted_iota(jnp.int32, (1, n * cache), 1)
    column_row = lax.div(column, cache)
    column_length = jnp.zeros_like(column)
    for r in range(n):
        column_length = jnp.where(column_row == r, lengths[r], column_length)
    usable = column - column_row * cache < column_length
    target = jnp.where(usable, column_row, -1)
    s_old = jnp.where(jnp.bitwise_and(row_old, n - 1) == target, s_old, low)
    row_new = lax.broadcasted_iota(jnp.int32, s_new.shape, 0)
    col_new = lax.broadcasted_iota(jnp.int32, s_new.shape, 1)
    same = jnp.bitwise_and(row_new, n - 1) == jnp.bitwise_and(col_new, n - 1)
    known = col_new <= jnp.bitwise_and(row_new, rows - 1)
    s_new = jnp.where(jnp.logical_and(same, known), s_new, low)
    highest = jnp.maximum(
        jnp.max(s_old, axis=1, keepdims=True), jnp.max(s_new, axis=1, keepdims=True)
    )
    e_old = jnp.exp(s_old - highest)
    e_new = jnp.exp(s_new - highest)
    denominator = jnp.sum(e_old, axis=1, keepdims=True) + jnp.sum(e_new, axis=1, keepdims=True)
    result = dot_nn((e_old / denominator).astype(jnp.bfloat16), vall[...])
    result = result + dot_nn((e_new / denominator).astype(jnp.bfloat16), fresh[1])
    result = result.astype(jnp.bfloat16)
    attended = jnp.concatenate(
        [result[h * rows : (h + 1) * rows, :] for h in range(heads)], axis=1
    )
    attall[d] = attended
    send(attall.at[d], attall.at[d], att_sems.at[0], att_sems.at[1], {"dp": other})

    al[:, :RANK] = against(attended, updated[2].astype(jnp.bfloat16))
    al[:, RANK:] = jnp.zeros((rows, LANES - RANK), jnp.float32)
    for k in range(1, n):
        send(al, al_recv.at[k - 1], al_sems.at[0], al_sems.at[1], {"tp": peers[k]})

    landed(wo, load_sem.at[6])
    landed(attall.at[other], att_sems.at[1])
    both = attall[...].reshape(2 * rows, width)

    def outputs(j, carry):
        for c in range(width // COLS):
            at = pl.ds(pl.multiple_of(j * width + c * COLS, COLS), COLS)
            block = dot_nn(both, wo[:, at]).astype(jnp.bfloat16)
            osrc[j, 0, :, c * COLS : (c + 1) * COLS] = block[:rows]
            osrc[j, 1, :, c * COLS : (c + 1) * COLS] = block[rows:]
        owner = half * d + j
        send(
            osrc.at[j, other],
            orecv.at[t],
            o_sems.at[0],
            o_sems.at[1],
            {"dp": other, "tp": owner},
        )
        mine = owner == t

        @pl.when(mine)
        def _():
            pltpu.make_async_copy(osrc.at[j, d], orecv.at[t], o_sems.at[1]).start()

        @pl.when(jnp.logical_not(mine))
        def _():
            send(osrc.at[j, d], orecv.at[t], o_sems.at[0], o_sems.at[1], {"tp": owner})

        return carry

    lax.fori_loop(0, half, outputs, 0)

    landed(al_recv, al_sems.at[1])
    inner = al[...]
    for k in range(n - 1):
        inner = inner + al_recv[k]
    lora = dot_nn(inner[:, :RANK].astype(jnp.bfloat16), updated[3].astype(jnp.bfloat16))

    landed(orecv, o_sems.at[1])
    total = adapter_scale_factor * lora
    for k in range(n):
        total = total + orecv[k].astype(jnp.float32)
    dec[...] = total.astype(jnp.bfloat16)
    pltpu.make_async_copy(dec, dec_out, out_sems.at[4]).start()

    landed(kall.at[pl.ds(0, (n - 1) * cache)], kv_send.at[0])
    landed(vall.at[pl.ds(0, (n - 1) * cache)], kv_send.at[1])
    for m in range(4):
        landed(rs.at[m], rs_send.at[m])
        landed(wfull.at[m, :, others], ag_send.at[m])
        landed(gs.at[m], g_send.at[m])
        landed(updated.at[m], out_sems.at[m])
    landed(dec, out_sems.at[4])
    landed(ne_recv, ne_sems.at[0])
    landed(small_recv, small_sems.at[0])
    landed(qr, q_sems.at[0])
    landed(attall.at[d], att_sems.at[0])
    landed(al_recv, al_sems.at[0])
    landed(orecv.at[pl.ds(0, n - 1)], o_sems.at[0])
    for k in range(n - 1):
        landed(states, st_sems.at[0])

    @pl.when(jnp.logical_not(stays))
    def _():
        landed(states, st_sems.at[0])
        landed(orecv.at[0], o_sems.at[0])


def hand_over(dec, factors, dec_out, qd, qu, od, ou, sems):
    copies = [pltpu.make_async_copy(dec, dec_out, sems.at[4])]
    for m, target in enumerate((qd, qu, od, ou)):
        copies.append(pltpu.make_async_copy(factors.at[m], target, sems.at[m]))
    for copy in copies:
        copy.start()
    for copy in copies:
        copy.wait()


def fused(
    query_inputs,
    output_inputs,
    query_cotangent,
    output_cotangent,
    completion,
    rewards,
    query_down,
    query_up,
    output_down,
    output_up,
    query_fixed_weight,
    output_fixed_weight,
    keyval_frozen,
    decode_states,
    key_cache,
    value_cache,
    cache_lengths,
):
    n = lax.axis_size("tp")
    tokens, width = query_inputs.shape
    steps_count, row_count, _ = decode_states.shape
    rows = steps_count * row_count
    cache = key_cache.shape[2]
    vmem = pl.BlockSpec(memory_space=pltpu.VMEM)
    smem = pl.BlockSpec(memory_space=pltpu.SMEM)
    hbm = pl.BlockSpec(memory_space=pl.ANY)
    bf16, f32 = jnp.bfloat16, jnp.float32
    dma = pltpu.SemaphoreType.DMA
    outs = pl.pallas_call(
        lambda *refs: fused_kernel(n, *refs),
        out_shape=(
            jax.ShapeDtypeStruct((rows, width), bf16),
            jax.ShapeDtypeStruct((4, RANK, width), f32),
        ),
        in_specs=[hbm] * 10 + [vmem, smem, smem] + [hbm] * 4,
        out_specs=(hbm, hbm),
        scratch_shapes=[
            pltpu.VMEM((rows, width), bf16),
            pltpu.VMEM((4, RANK, width), f32),
            pltpu.VMEM((4, RANK, width), f32),
            pltpu.VMEM((rows, width), bf16),
            pltpu.VMEM((4, tokens, width), bf16),
            pltpu.VMEM(query_fixed_weight.shape, bf16),
            pltpu.VMEM(output_fixed_weight.shape, bf16),
            pltpu.VMEM(keyval_frozen.shape, bf16),
            pltpu.VMEM((4, RANK, width), bf16),
            pltpu.VMEM((4, n, RANK, LANES), bf16),
            pltpu.VMEM((4, n - 1, RANK, LANES), bf16),
            pltpu.VMEM((4, RANK, LANES), bf16),
            pltpu.VMEM((4, RANK, tokens), bf16),
            pltpu.VMEM((4, RANK, width), bf16),
            pltpu.VMEM((4, RANK, width), bf16),
            pltpu.VMEM((4, RANK, width), f32),
            pltpu.VMEM((n * cache, HD), bf16),
            pltpu.VMEM((n * cache, HD), bf16),
            pltpu.VMEM((n, 2, rows, HD), bf16),
            pltpu.VMEM((n - 1, 2, rows, HD), bf16),
            pltpu.VMEM((n // 2, 2 * rows, width), bf16),
            pltpu.VMEM((rows + 8, LANES), f32),
            pltpu.VMEM((n - 1, rows + 8, LANES), f32),
            pltpu.VMEM((2, rows, width), f32),
            pltpu.VMEM((rows, width), f32),
            pltpu.VMEM((2, rows, width), bf16),
            pltpu.VMEM((rows, LANES), f32),
            pltpu.VMEM((n - 1, rows, LANES), f32),
            pltpu.VMEM((n // 2, 2, rows, width), bf16),
            pltpu.VMEM((n, rows, width), bf16),
            dma((14,)),
            dma((2,)),
            dma((2,)),
            dma((4,)),
            dma((4,)),
            dma((4,)),
            dma((4,)),
            dma((2,)),
            dma((2,)),
            dma((4,)),
            dma((4,)),
            dma((2,)),
            dma((2,)),
            dma((2,)),
            dma((2,)),
            dma((2,)),
            dma((5,)),
        ],
        compiler_params=pltpu.CompilerParams(
            collective_id=0, has_side_effects=True, vmem_limit_bytes=56 << 20
        ),
        cost_estimate=pl.CostEstimate(
            flops=4 * 10**9, bytes_accessed=36 * 10**6, transcendentals=1 << 17
        ),
    )(
        query_inputs,
        query_cotangent,
        output_inputs,
        output_cotangent,
        query_fixed_weight,
        output_fixed_weight,
        keyval_frozen,
        decode_states.reshape(rows, width),
        key_cache[0],
        value_cache[0],
        completion.reshape(n, 1, tokens // n),
        rewards,
        cache_lengths,
        query_down.T,
        query_up,
        output_down.T,
        output_up,
    )
    final = pl.pallas_call(
        hand_over,
        out_shape=(
            jax.ShapeDtypeStruct((rows, width), bf16),
            *[jax.ShapeDtypeStruct((RANK, width), f32)] * 4,
        ),
        in_specs=[hbm, hbm],
        out_specs=(hbm,) * 5,
        scratch_shapes=[dma((5,))],
    )(*outs)
    decoded = final[0].reshape(steps_count, row_count, width)
    return (decoded, final[1].T, final[2], final[3].T, final[4])


def fits(mesh):
    return mesh.shape["dp"] == 2 and mesh.shape["tp"] == KVH


def solution(mesh):
    return jax.shard_map(
        fused if fits(mesh) else on_device,
        mesh=mesh,
        in_specs=(
            P(("grp", "dp"), "tp"),
            P(("grp", "dp"), "tp"),
            P(("grp", "dp"), "tp"),
            P(("grp", "dp"), "tp"),
            P(("grp", "dp")),
            P("grp"),
            P(("grp", "tp"), None),
            P("grp", "tp"),
            P(("grp", "tp"), None),
            P("grp", "tp"),
            P("dp", "tp"),
            P("tp", "dp"),
            P("tp", None),
            P(None, ("grp", "dp"), "tp"),
            P(("grp", "dp", "tp"), None, None, None),
            P(("grp", "dp", "tp"), None, None, None),
            P(("grp", "dp")),
        ),
        out_specs=(
            P(None, ("grp", "dp"), "tp"),
            P(("grp", "tp"), None),
            P("grp", "tp"),
            P(("grp", "tp"), None),
            P("grp", "tp"),
        ),
        check_vma=False,
    )
```

```python
import math

import jax
import jax.numpy as jnp
from jax import lax
from jax.experimental import pallas as pl
from jax.experimental.pallas import tpu as pltpu
from jax.sharding import PartitionSpec as P

HEADS = 64
KVH = 8
HD = 128


adapter_scale_factor = 2.0
learn_rate = 8.0
clip_norm = 1.0


def attend(queries, cache_keys, cache_values, new_keys, new_values, valid_lengths, decode_step):
    score_scale = 1.0 / math.sqrt(queries.shape[-1])
    s_cache = (
        jnp.einsum("bgmd,bgcd->bgmc", queries, cache_keys, preferred_element_type=jnp.float32)
        * score_scale
    )
    s_new = (
        jnp.einsum("bgmd,bsgd->bgms", queries, new_keys, preferred_element_type=jnp.float32)
        * score_scale
    )
    cache_ok = (jnp.arange(cache_keys.shape[2], dtype=jnp.int32)[None, :] < valid_lengths[:, None])[
        :, None, None, :
    ]
    new_ok = (jnp.arange(new_keys.shape[1], dtype=jnp.int32) <= decode_step)[None, None, None, :]
    s_cache = jnp.where(cache_ok, s_cache, -jnp.inf)
    s_new = jnp.where(new_ok, s_new, -jnp.inf)
    highest = jnp.maximum(jnp.max(s_cache, axis=-1), jnp.max(s_new, axis=-1))[..., None]
    e_cache = jnp.exp(s_cache - highest)
    e_new = jnp.exp(s_new - highest)
    denominator = jnp.sum(e_cache, axis=-1, keepdims=True) + jnp.sum(e_new, axis=-1, keepdims=True)
    p_cache = (e_cache / denominator).astype(jnp.bfloat16)
    p_new = (e_new / denominator).astype(jnp.bfloat16)
    result = jnp.einsum(
        "bgmc,bgcd->bgmd", p_cache, cache_values, preferred_element_type=jnp.float32
    )
    result = result + jnp.einsum(
        "bgms,bsgd->bgmd", p_new, new_values, preferred_element_type=jnp.float32
    )
    return result.astype(jnp.bfloat16)


def weighted(token_weight, values_in):
    return (token_weight[:, None] * values_in).astype(jnp.bfloat16)


def across(left, right):
    return lax.dot_general(
        left, right, (((0,), (0,)), ((), ())), preferred_element_type=jnp.float32
    )


def against(left, right):
    return lax.dot_general(
        left, right, (((1,), (1,)), ((), ())), preferred_element_type=jnp.float32
    )


def squares(gradients):
    return sum((jnp.sum(gradient * gradient) for gradient in gradients))


def on_device(
    query_inputs,
    output_inputs,
    query_cotangent,
    output_cotangent,
    completion,
    rewards,
    query_down,
    query_up,
    output_down,
    output_up,
    query_fixed_weight,
    output_fixed_weight,
    keyval_frozen,
    decode_states,
    key_cache,
    value_cache,
    cache_lengths,
):
    advantage = rewards - jnp.mean(rewards)
    labels = jnp.arange(rewards.shape[0], dtype=jnp.int32)
    token_weight = jnp.sum(
        jnp.where(completion[:, None] == labels[None, :], advantage[None, :], 0.0), axis=1
    )
    down_q = query_down.astype(jnp.bfloat16)
    up_q = query_up.astype(jnp.bfloat16)
    down_o = output_down.astype(jnp.bfloat16)
    up_o = output_up.astype(jnp.bfloat16)
    partials = (
        jnp.dot(query_inputs, down_q, preferred_element_type=jnp.float32),
        against(query_cotangent, up_q),
        jnp.dot(output_inputs, down_o, preferred_element_type=jnp.float32),
        against(output_cotangent, up_o),
    )
    inner_query, back_query, inner_output, back_output = (
        lax.psum(partials[0].astype(jnp.bfloat16), "tp").astype(jnp.float32),
        lax.psum(partials[1].astype(jnp.bfloat16), "tp").astype(jnp.float32),
        lax.psum(partials[2].astype(jnp.bfloat16), "tp").astype(jnp.float32),
        lax.psum(partials[3].astype(jnp.bfloat16), "tp").astype(jnp.float32),
    )
    terms = (
        across(query_inputs, weighted(token_weight, back_query)),
        across(query_cotangent, weighted(token_weight, inner_query)),
        across(output_inputs, weighted(token_weight, back_output)),
        across(output_cotangent, weighted(token_weight, inner_output)),
    )
    current = (query_down, query_up.T, output_down, output_up.T)
    gradients = (
        lax.psum(terms[0].astype(jnp.bfloat16), "dp").astype(jnp.float32),
        lax.psum(terms[1].astype(jnp.bfloat16), "dp").astype(jnp.float32),
        lax.psum(terms[2].astype(jnp.bfloat16), "dp").astype(jnp.float32),
        lax.psum(terms[3].astype(jnp.bfloat16), "dp").astype(jnp.float32),
    )
    total_sq = lax.psum(squares(gradients), "tp")
    shrink = clip_norm / (jnp.sqrt(total_sq) + 1e-06)
    updated = tuple(
        (
            factor_state - learn_rate * shrink * gradient
            for factor_state, gradient in zip(current, gradients)
        )
    )
    new_query_down = updated[0]
    new_query_up = updated[1].T
    new_output_down = updated[2]
    new_output_up = updated[3].T
    rollout_down_q = new_query_down.astype(jnp.bfloat16)
    rollout_up_q = new_query_up.astype(jnp.bfloat16)
    rollout_down_o = new_output_down.astype(jnp.bfloat16)
    rollout_up_o = new_output_up.astype(jnp.bfloat16)
    full_down_q, full_up_o = (
        lax.all_gather(rollout_down_q, "tp", axis=0, tiled=True),
        lax.all_gather(rollout_up_o, "tp", axis=1, tiled=True),
    )
    steps_count, row_count, local_width = decode_states.shape
    query_width = query_fixed_weight.shape[1]
    tp_count = lax.axis_size("tp")
    tp_rank = lax.axis_index("tp")
    adapter_weight_delta = jnp.dot(full_down_q, rollout_up_q, preferred_element_type=jnp.float32)
    query_combined_weight = (
        lax.all_gather(query_fixed_weight, "dp", axis=0, tiled=True).astype(jnp.float32)
        + adapter_scale_factor * adapter_weight_delta
    ).astype(jnp.bfloat16)
    adapter_weight_delta = jnp.dot(rollout_down_o, full_up_o, preferred_element_type=jnp.float32)
    output_combined_weight = (
        lax.all_gather(output_fixed_weight, "dp", axis=1, tiled=True).astype(jnp.float32)
        + adapter_scale_factor * adapter_weight_delta
    ).astype(jnp.bfloat16)
    queries = jnp.einsum(
        "srd,dh->srh",
        lax.all_gather(decode_states, "tp", axis=2, tiled=True),
        query_combined_weight,
        preferred_element_type=jnp.float32,
    ).astype(jnp.bfloat16)
    fresh_part = jnp.einsum(
        "srd,dk->srk", decode_states, keyval_frozen, preferred_element_type=jnp.float32
    )
    part_heads = query_width // HD
    group_heads = HEADS // KVH
    new_entries = lax.psum(fresh_part.astype(jnp.bfloat16), "tp")
    kv_head = tp_rank * part_heads // group_heads
    own_keys = lax.dynamic_slice_in_dim(new_entries, kv_head * HD, HD, 2)
    own_values = lax.dynamic_slice_in_dim(new_entries, (KVH + kv_head) * HD, HD, 2)
    copies = tp_count // KVH
    spread_keys = jnp.repeat(key_cache, copies, axis=1)
    spread_values = jnp.repeat(value_cache, copies, axis=1)
    head_keys, head_values = (
        lax.all_to_all(spread_keys, "tp", split_axis=1, concat_axis=0, tiled=True),
        lax.all_to_all(spread_values, "tp", split_axis=1, concat_axis=0, tiled=True),
    )
    query_heads = queries.reshape(steps_count, row_count, 1, part_heads, HD)
    step_keys = jnp.transpose(own_keys, (1, 0, 2))[:, :, None, :]
    step_values = jnp.transpose(own_values, (1, 0, 2))[:, :, None, :]
    results = [
        attend(
            query_heads[decode_step],
            head_keys,
            head_values,
            step_keys,
            step_values,
            cache_lengths,
            decode_step,
        )
        for decode_step in range(steps_count)
    ]
    attended = jnp.stack(results).reshape(steps_count, row_count, query_width)
    flattened = attended.reshape(steps_count * row_count, query_width)
    local_columns = output_combined_weight.shape[1] // tp_count
    summed_out = lax.psum_scatter(
        lax.dot_general(
            output_combined_weight,
            flattened,
            (((0,), (1,)), ((), ())),
            preferred_element_type=jnp.float32,
        ).astype(jnp.bfloat16),
        "tp",
        scatter_dimension=0,
        tiled=True,
    ).astype(jnp.float32)
    decoded = summed_out.T.reshape(steps_count, row_count, local_columns).astype(jnp.bfloat16)
    return (decoded, new_query_down, new_query_up, new_output_down, new_output_up)


MESH = pl.DeviceIdType.MESH
RANK = 64
LANES = 128
COLS = 256


def dot_nn(left, right):
    return jnp.dot(left, right, preferred_element_type=jnp.float32)


def landed(ref, sem):
    pltpu.make_async_copy(ref, ref, sem).wait()


def fused_kernel(
    n,
    xq,
    cq,
    xo,
    co,
    wq_hbm,
    wo_hbm,
    kv_hbm,
    states_hbm,
    kc,
    vc,
    completion,
    rewards,
    lengths,
    qd_hbm,
    qu_hbm,
    od_hbm,
    ou_hbm,
    dec_out,
    new_out,
    states,
    held,
    updated,
    dec,
    act,
    wq,
    wo,
    kv,
    columns,
    part,
    pair_part,
    line_part,
    rs,
    own_w,
    wfull,
    gs,
    gr,
    gsum,
    kall,
    vall,
    ne_src,
    ne_recv,
    stf,
    small,
    small_recv,
    qp,
    qr,
    attall,
    al,
    al_recv,
    opair,
    opair_recv,
    osum,
    orecv,
    load_sem,
    kv_send,
    kv_recv,
    pair_send,
    pair_recv,
    rs_send,
    rs_recv,
    ag_send,
    ag_line,
    ag_pair,
    ne_sems,
    st_sems,
    g_send,
    g_recv,
    small_sems,
    q_sems,
    att_sems,
    al_sems,
    opair_send,
    opair_got,
    o_sems,
    out_sems,
):
    d = lax.axis_index("dp")
    t = lax.axis_index("tp")
    other = 1 - d
    half = n // 2
    width = act.shape[2]
    rows = states.shape[0]
    cache = kc.shape[1]
    peers = [lax.rem(t + k, n) for k in range(n)]
    y = lax.rem(t, 2)
    z = lax.div(t, 2)
    pair = t + 1 - 2 * y
    line = [lax.rem(t + 2 * k, n) for k in range(half)]
    line_z = [lax.rem(z + k, half) for k in range(half)]

    def load(source, target, index):
        pltpu.make_async_copy(source, target, load_sem.at[index]).start()

    def send(source, target, send_sem, recv_sem, device):
        pltpu.make_async_remote_copy(
            src_ref=source,
            dst_ref=target,
            send_sem=send_sem,
            recv_sem=recv_sem,
            device_id=device,
            device_id_type=MESH,
        ).start()

    load(states_hbm, states, 7)
    for index, source in enumerate((qd_hbm, qu_hbm, od_hbm, ou_hbm)):
        load(source, held.at[index], 8 + index)
    for index, source in enumerate((xq, cq, xo, co)):
        load(source, act.at[index], index)
    load(kv_hbm, kv, 4)

    barrier = pltpu.get_barrier_semaphore()
    for k in range(n):
        if k > 0:
            pl.semaphore_signal(barrier, inc=1, device_id={"tp": peers[k]}, device_id_type=MESH)
        pl.semaphore_signal(
            barrier, inc=1, device_id={"dp": other, "tp": peers[k]}, device_id_type=MESH
        )

    for m in range(4):
        landed(held.at[m], load_sem.at[8 + m])
        columns[m] = held[m].T.astype(jnp.bfloat16)
    count = rewards.shape[0]
    mean = rewards[0]
    for c in range(1, count):
        mean = mean + rewards[c]
    mean = mean / count
    own_completion = completion[t]
    token_weight = jnp.zeros(own_completion.shape, jnp.float32)
    for c in range(count):
        token_weight = jnp.where(own_completion == c, rewards[c] - mean, token_weight)

    pl.semaphore_wait(barrier, 2 * n - 1)

    home = lax.div(t, half)
    stays = home == d
    st_place = stf.at[lax.rem(t, half), pl.ds(pl.multiple_of(d * rows, rows), rows)]
    for k in range(1, half):
        send(states_hbm, st_place, st_sems.at[0], st_sems.at[1], {"dp": home, "tp": line[k]})

    @pl.when(stays)
    def _():
        pltpu.make_async_copy(states_hbm, st_place, st_sems.at[1]).start()

    @pl.when(jnp.logical_not(stays))
    def _():
        send(states_hbm, st_place, st_sems.at[0], st_sems.at[1], {"dp": other})

    def project(m, carry):
        landed(act.at[m], load_sem.at[m])
        for c in range(width // COLS):
            block = dot_nn(act[m, c * COLS : (c + 1) * COLS, :], columns[m])
            block = block.T.astype(jnp.bfloat16)
            for i in range(COLS // LANES):
                part[m, i, c] = block[:, i * LANES : (i + 1) * LANES]
        send(part.at[m, 1 - y], pair_part.at[m], pair_send.at[m], pair_recv.at[m], {"tp": pair})
        return carry

    def pair_sum(m):
        landed(pair_part.at[m], pair_recv.at[m])
        for i in range(half):
            total = part[m, y, i].astype(jnp.float32) + pair_part[m, i].astype(jnp.float32)
            line_part[m, i] = total.astype(jnp.bfloat16)
        for k in range(1, half):
            send(
                line_part.at[m, line_z[k]],
                rs.at[m, k - 1],
                rs_send.at[m],
                rs_recv.at[m],
                {"tp": line[k]},
            )

    def project_and_sum(m, carry):
        project(m, carry)
        pair_sum(m - 1)
        return carry

    project(0, 0)
    load(wq_hbm, wq, 5)
    load(wo_hbm, wo, 6)
    lax.fori_loop(1, 4, project_and_sum, 0)
    pair_sum(3)
    landed(stf.at[pl.ds(0, half // 2)], st_sems.at[1])
    for i in range(half // 2):
        place = stf.at[2 * i + y]
        send(place, place, st_sems.at[2], st_sems.at[3], {"tp": pair})

    landed(states, load_sem.at[7])
    landed(kv, load_sem.at[4])
    for c in range(2 * n * HD // COLS):
        block = dot_nn(states[...], kv[:, c * COLS : (c + 1) * COLS]).astype(jnp.bfloat16)
        for i in range(COLS // HD):
            head = c * (COLS // HD) + i
            ne_src[head % n, head // n] = block[:, i * HD : (i + 1) * HD]

    def tokens_of(owner):
        return pl.ds(pl.multiple_of(owner * LANES, LANES), LANES)

    def reduce_weight(m):
        landed(rs.at[m], rs_recv.at[m])
        total = line_part[m, z].astype(jnp.float32)
        for k in range(half - 1):
            total = total + rs[m, k].astype(jnp.float32)
        block = (total * token_weight).astype(jnp.bfloat16)
        own_w[m] = block
        place = wfull.at[m, :, tokens_of(t)]
        wfull[m, :, tokens_of(t)] = block
        for k in range(1, half):
            send(own_w.at[m], place, ag_send.at[m], ag_line.at[m], {"tp": line[k]})
        send(own_w.at[m], place, ag_send.at[m], ag_pair.at[m], {"tp": pair})

    def forward(m):
        landed(wfull.at[m, :, pl.ds(0, (half - 1) * LANES)], ag_line.at[m])
        for k in range(1, half):
            place = wfull.at[m, :, tokens_of(line[k])]
            send(place, place, ag_send.at[m], ag_pair.at[m], {"tp": pair})

    def weight_and_forward(m, carry):
        reduce_weight(m)
        forward(m - 1)
        return carry

    reduce_weight(0)
    lax.fori_loop(1, 4, weight_and_forward, 0)
    forward(3)

    for k in range(1, n):
        send(ne_src.at[peers[k]], ne_recv.at[k - 1], ne_sems.at[0], ne_sems.at[1], {"tp": peers[k]})

    own_cache = pl.ds(pl.multiple_of(t * cache, cache), cache)
    for k in range(1, n):
        send(kc.at[peers[k]], kall.at[own_cache], kv_send.at[0], kv_recv.at[0], {"tp": peers[k]})
        send(vc.at[peers[k]], vall.at[own_cache], kv_send.at[1], kv_recv.at[1], {"tp": peers[k]})
    load(kc.at[t], kall.at[own_cache], 12)
    load(vc.at[t], vall.at[own_cache], 13)

    others = pl.ds(0, (n - 1) * LANES)

    def gradient(i, carry):
        m = i + 1 - 2 * lax.rem(i, 2)
        landed(wfull.at[i, :, pl.ds(0, half * LANES)], ag_pair.at[i])
        for c in range(width // COLS):
            at = slice(c * COLS, (c + 1) * COLS)
            gs[m, :, at] = dot_nn(wfull[i], act[m, :, at]).astype(jnp.bfloat16)
        send(gs.at[m], gr.at[m], g_send.at[m], g_recv.at[m], {"dp": other})
        return carry

    lax.fori_loop(0, 4, gradient, 0)

    squared = jnp.zeros((8, LANES), jnp.float32)
    for m in (1, 0, 3, 2):
        landed(gr.at[m], g_recv.at[m])
        total = gs[m].astype(jnp.float32) + gr[m].astype(jnp.float32)
        gsum[m] = total
        square = total * total
        for a in range(RANK // 8):
            for b in range(width // LANES):
                squared = squared + square[a * 8 : (a + 1) * 8, b * LANES : (b + 1) * LANES]
    small[:rows, :RANK] = against(states[...], gsum[0].astype(jnp.bfloat16))
    small[:rows, RANK:] = dot_nn(states[...], columns[0])
    small[rows:, :] = squared
    for k in range(1, n):
        send(small, small_recv.at[k - 1], small_sems.at[0], small_sems.at[1], {"tp": peers[k]})

    landed(stf.at[pl.ds(0, half // 2)], st_sems.at[3])
    landed(wq, load_sem.at[5])

    def queries(c, carry):
        at = pl.ds(pl.multiple_of(c * COLS, COLS), COLS)
        total = dot_nn(stf[0], wq[0:width, at])
        for j in range(1, half):
            total = total + dot_nn(stf[j], wq[j * width : (j + 1) * width, at])
        qp[0, :, at] = total[:rows]
        qp[1, :, at] = total[rows:]
        return carry

    lax.fori_loop(0, width // COLS, queries, 0)
    send(qp.at[other], qr, q_sems.at[0], q_sems.at[1], {"dp": other})

    landed(ne_recv, ne_sems.at[1])
    fresh = ne_src[t].astype(jnp.float32)
    for k in range(n - 1):
        fresh = fresh + ne_recv[k].astype(jnp.float32)
    fresh = fresh.astype(jnp.bfloat16)

    landed(small_recv, small_sems.at[1])
    total = small[...]
    for k in range(n - 1):
        total = total + small_recv[k]
    norm = jnp.sqrt(jnp.sum(total[rows:, :], axis=(0, 1), keepdims=True))
    step = learn_rate * (clip_norm / (norm + 1e-06))
    for m in range(4):
        updated[m] = held[m] - step * gsum[m]
        pltpu.make_async_copy(updated.at[m], new_out.at[m], out_sems.at[m]).start()
    inner = (total[:rows, RANK:] - step * total[:rows, :RANK]).astype(jnp.bfloat16)
    lora = dot_nn(inner, updated[1].astype(jnp.bfloat16))

    landed(qr, q_sems.at[1])
    query = (qp[d] + qr[...] + adapter_scale_factor * lora).astype(jnp.bfloat16)
    heads = width // HD
    stacked = jnp.concatenate([query[:, h * HD : (h + 1) * HD] for h in range(heads)], axis=0)

    landed(kall.at[own_cache], load_sem.at[12])
    landed(vall.at[own_cache], load_sem.at[13])
    landed(kall.at[pl.ds(0, (n - 1) * cache)], kv_recv.at[0])
    landed(vall.at[pl.ds(0, (n - 1) * cache)], kv_recv.at[1])
    scale = 1.0 / math.sqrt(HD)
    low = jnp.float32(-1e30)
    s_old = against(stacked, kall[...]) * scale
    s_new = against(stacked, fresh[0]) * scale
    row_old = lax.broadcasted_iota(jnp.int32, s_old.shape, 0)
    column = lax.broadcasted_iota(jnp.int32, (1, n * cache), 1)
    column_row = lax.div(column, cache)
    column_length = jnp.zeros_like(column)
    for r in range(n):
        column_length = jnp.where(column_row == r, lengths[r], column_length)
    usable = column - column_row * cache < column_length
    target = jnp.where(usable, column_row, -1)
    s_old = jnp.where(jnp.bitwise_and(row_old, n - 1) == target, s_old, low)
    row_new = lax.broadcasted_iota(jnp.int32, s_new.shape, 0)
    col_new = lax.broadcasted_iota(jnp.int32, s_new.shape, 1)
    same = jnp.bitwise_and(row_new, n - 1) == jnp.bitwise_and(col_new, n - 1)
    known = col_new <= jnp.bitwise_and(row_new, rows - 1)
    s_new = jnp.where(jnp.logical_and(same, known), s_new, low)
    highest = jnp.maximum(
        jnp.max(s_old, axis=1, keepdims=True), jnp.max(s_new, axis=1, keepdims=True)
    )
    e_old = jnp.exp(s_old - highest)
    e_new = jnp.exp(s_new - highest)
    denominator = jnp.sum(e_old, axis=1, keepdims=True) + jnp.sum(e_new, axis=1, keepdims=True)
    inverse = 1.0 / denominator
    result = dot_nn((e_old * inverse).astype(jnp.bfloat16), vall[...])
    result = result + dot_nn((e_new * inverse).astype(jnp.bfloat16), fresh[1])
    result = result.astype(jnp.bfloat16)
    attended = jnp.concatenate(
        [result[h * rows : (h + 1) * rows, :] for h in range(heads)], axis=1
    )
    attall[d] = attended
    send(attall.at[d], attall.at[d], att_sems.at[0], att_sems.at[1], {"dp": other})

    al[:, :RANK] = against(attended, updated[2].astype(jnp.bfloat16))
    al[:, RANK:] = jnp.zeros((rows, LANES - RANK), jnp.float32)
    for k in range(1, n):
        send(al, al_recv.at[k - 1], al_sems.at[0], al_sems.at[1], {"tp": peers[k]})

    landed(wo, load_sem.at[6])
    landed(attall.at[other], att_sems.at[1])
    both = attall[...].reshape(2 * rows, width)

    def product(j, c):
        at = pl.ds(pl.multiple_of(j * width + c * COLS, COLS), COLS)
        return dot_nn(both, wo[:, at])

    def for_pair(i, carry):
        for c in range(width // COLS):
            at = slice(c * COLS, (c + 1) * COLS)
            opair[i, :, at] = product(2 * i + 1 - y, c).astype(jnp.bfloat16)
        send(opair.at[i], opair_recv.at[i], opair_send.at[i], opair_got.at[i], {"tp": pair})
        return carry

    lax.fori_loop(0, half // 2, for_pair, 0)

    def for_line(i, carry):
        landed(opair_recv.at[i], opair_got.at[i])
        for c in range(width // COLS):
            at = slice(c * COLS, (c + 1) * COLS)
            block = product(2 * i + y, c).astype(jnp.bfloat16).astype(jnp.float32)
            block = (block + opair_recv[i, :, at].astype(jnp.float32)).astype(jnp.bfloat16)
            osum[i, 0, :, at] = block[:rows]
            osum[i, 1, :, at] = block[rows:]
        owner = half * d + 2 * i + y
        send(
            osum.at[i, other],
            orecv.at[z],
            o_sems.at[0],
            o_sems.at[1],
            {"dp": other, "tp": owner},
        )
        mine = owner == t

        @pl.when(mine)
        def _():
            pltpu.make_async_copy(osum.at[i, d], orecv.at[z], o_sems.at[1]).start()

        @pl.when(jnp.logical_not(mine))
        def _():
            send(osum.at[i, d], orecv.at[z], o_sems.at[0], o_sems.at[1], {"tp": owner})

        return carry

    lax.fori_loop(0, half // 2, for_line, 0)

    landed(al_recv, al_sems.at[1])
    inner = al[...]
    for k in range(n - 1):
        inner = inner + al_recv[k]
    lora = dot_nn(inner[:, :RANK].astype(jnp.bfloat16), updated[3].astype(jnp.bfloat16))

    landed(orecv, o_sems.at[1])
    total = adapter_scale_factor * lora
    for k in range(half):
        total = total + orecv[k].astype(jnp.float32)
    dec[...] = total.astype(jnp.bfloat16)
    pltpu.make_async_copy(dec, dec_out, out_sems.at[4]).start()

    landed(kall.at[pl.ds(0, (n - 1) * cache)], kv_send.at[0])
    landed(vall.at[pl.ds(0, (n - 1) * cache)], kv_send.at[1])
    for m in range(4):
        landed(pair_part.at[m], pair_send.at[m])
        landed(rs.at[m], rs_send.at[m])
        landed(wfull.at[m, :, others], ag_send.at[m])
        landed(gs.at[m], g_send.at[m])
        landed(updated.at[m], out_sems.at[m])
    landed(dec, out_sems.at[4])
    landed(ne_recv, ne_sems.at[0])
    landed(small_recv, small_sems.at[0])
    landed(qr, q_sems.at[0])
    landed(attall.at[d], att_sems.at[0])
    landed(al_recv, al_sems.at[0])
    for i in range(half // 2):
        landed(opair.at[i], opair_send.at[i])
    landed(orecv.at[pl.ds(0, half - 1)], o_sems.at[0])
    landed(stf.at[pl.ds(0, half // 2)], st_sems.at[2])
    for k in range(half - 1):
        landed(states, st_sems.at[0])

    @pl.when(jnp.logical_not(stays))
    def _():
        landed(states, st_sems.at[0])
        landed(orecv.at[0], o_sems.at[0])


def hand_over(dec, factors, dec_out, qd, qu, od, ou):
    dec_out[...] = dec[...]
    for m, target in enumerate((qd, qu, od, ou)):
        target[...] = factors[m]


def fused(
    query_inputs,
    output_inputs,
    query_cotangent,
    output_cotangent,
    completion,
    rewards,
    query_down,
    query_up,
    output_down,
    output_up,
    query_fixed_weight,
    output_fixed_weight,
    keyval_frozen,
    decode_states,
    key_cache,
    value_cache,
    cache_lengths,
):
    n = lax.axis_size("tp")
    tokens, width = query_inputs.shape
    steps_count, row_count, _ = decode_states.shape
    rows = steps_count * row_count
    cache = key_cache.shape[2]
    vmem = pl.BlockSpec(memory_space=pltpu.VMEM)
    smem = pl.BlockSpec(memory_space=pltpu.SMEM)
    hbm = pl.BlockSpec(memory_space=pl.ANY)
    bf16, f32 = jnp.bfloat16, jnp.float32
    dma = pltpu.SemaphoreType.DMA
    outs = pl.pallas_call(
        lambda *refs: fused_kernel(n, *refs),
        out_shape=(
            jax.ShapeDtypeStruct((rows, width), bf16),
            jax.ShapeDtypeStruct((4, RANK, width), f32),
        ),
        in_specs=[hbm] * 10 + [vmem, smem, smem] + [hbm] * 4,
        out_specs=(hbm, hbm),
        scratch_shapes=[
            pltpu.VMEM((rows, width), bf16),
            pltpu.VMEM((4, RANK, width), f32),
            pltpu.VMEM((4, RANK, width), f32),
            pltpu.VMEM((rows, width), bf16),
            pltpu.VMEM((4, tokens, width), bf16),
            pltpu.VMEM(query_fixed_weight.shape, bf16),
            pltpu.VMEM(output_fixed_weight.shape, bf16),
            pltpu.VMEM(keyval_frozen.shape, bf16),
            pltpu.VMEM((4, width, RANK), bf16),
            pltpu.VMEM((4, 2, n // 2, RANK, LANES), bf16),
            pltpu.VMEM((4, n // 2, RANK, LANES), bf16),
            pltpu.VMEM((4, n // 2, RANK, LANES), bf16),
            pltpu.VMEM((4, n // 2 - 1, RANK, LANES), bf16),
            pltpu.VMEM((4, RANK, LANES), bf16),
            pltpu.VMEM((4, RANK, tokens), bf16),
            pltpu.VMEM((4, RANK, width), bf16),
            pltpu.VMEM((4, RANK, width), bf16),
            pltpu.VMEM((4, RANK, width), f32),
            pltpu.VMEM((n * cache, HD), bf16),
            pltpu.VMEM((n * cache, HD), bf16),
            pltpu.VMEM((n, 2, rows, HD), bf16),
            pltpu.VMEM((n - 1, 2, rows, HD), bf16),
            pltpu.VMEM((n // 2, 2 * rows, width), bf16),
            pltpu.VMEM((rows + 8, LANES), f32),
            pltpu.VMEM((n - 1, rows + 8, LANES), f32),
            pltpu.VMEM((2, rows, width), f32),
            pltpu.VMEM((rows, width), f32),
            pltpu.VMEM((2, rows, width), bf16),
            pltpu.VMEM((rows, LANES), f32),
            pltpu.VMEM((n - 1, rows, LANES), f32),
            pltpu.VMEM((n // 4, 2 * rows, width), bf16),
            pltpu.VMEM((n // 4, 2 * rows, width), bf16),
            pltpu.VMEM((n // 4, 2, rows, width), bf16),
            pltpu.VMEM((n // 2, rows, width), bf16),
            dma((14,)),
            dma((2,)),
            dma((2,)),
            dma((4,)),
            dma((4,)),
            dma((4,)),
            dma((4,)),
            dma((4,)),
            dma((4,)),
            dma((4,)),
            dma((2,)),
            dma((4,)),
            dma((4,)),
            dma((4,)),
            dma((2,)),
            dma((2,)),
            dma((2,)),
            dma((2,)),
            dma((2,)),
            dma((2,)),
            dma((2,)),
            dma((5,)),
        ],
        compiler_params=pltpu.CompilerParams(
            collective_id=0, has_side_effects=True, vmem_limit_bytes=56 << 20
        ),
        cost_estimate=pl.CostEstimate(
            flops=4 * 10**9, bytes_accessed=36 * 10**6, transcendentals=1 << 17
        ),
    )(
        query_inputs,
        query_cotangent,
        output_inputs,
        output_cotangent,
        query_fixed_weight,
        output_fixed_weight,
        keyval_frozen,
        decode_states.reshape(rows, width),
        key_cache[0],
        value_cache[0],
        completion.reshape(n, 1, tokens // n),
        rewards,
        cache_lengths,
        query_down.T,
        query_up,
        output_down.T,
        output_up,
    )
    final = pl.pallas_call(
        hand_over,
        out_shape=(
            jax.ShapeDtypeStruct((rows, width), bf16),
            *[jax.ShapeDtypeStruct((RANK, width), f32)] * 4,
        ),
        in_specs=[vmem, vmem],
        out_specs=(vmem,) * 5,
    )(*outs)
    decoded = final[0].reshape(steps_count, row_count, width)
    return (decoded, final[1].T, final[2], final[3].T, final[4])


def fits(mesh):
    return mesh.shape["dp"] == 2 and mesh.shape["tp"] == KVH


def solution(mesh):
    return jax.shard_map(
        fused if fits(mesh) else on_device,
        mesh=mesh,
        in_specs=(
            P(("grp", "dp"), "tp"),
            P(("grp", "dp"), "tp"),
            P(("grp", "dp"), "tp"),
            P(("grp", "dp"), "tp"),
            P(("grp", "dp")),
            P("grp"),
            P(("grp", "tp"), None),
            P("grp", "tp"),
            P(("grp", "tp"), None),
            P("grp", "tp"),
            P("dp", "tp"),
            P("tp", "dp"),
            P("tp", None),
            P(None, ("grp", "dp"), "tp"),
            P(("grp", "dp", "tp"), None, None, None),
            P(("grp", "dp", "tp"), None, None, None),
            P(("grp", "dp")),
        ),
        out_specs=(
            P(None, ("grp", "dp"), "tp"),
            P(("grp", "tp"), None),
            P("grp", "tp"),
            P(("grp", "tp"), None),
            P("grp", "tp"),
        ),
        check_vma=False,
    )
```
